1024 devices in a mesh: ep: 32 (over x, y, core), dp: 32 (over z).
Axes of the slice: x: 4, y: 4, z: 32, core: 2. Of those that a mesh axis runs over, the one named last changes fastest.
Arguments:
- cotangent: bfloat16 [131072, 2048], P(('ep', 'dp')), may hold values from -6 to 6
- route_ids: int32 [131072, 2], P(('ep', 'dp')), may hold values from 0 to 31, all different within a row; in each aligned block of 128 rows (0 to 127, 128 to 255, ...) at most 10 rows name the same one
- route_probs: float32 [131072, 2], P(('ep', 'dp')), may hold values from 0.05 to 0.8
- expert_hidden: bfloat16 [327680, 768], P(('ep', 'dp')), may hold values from -6 to 6
- down_weight: bfloat16 [32, 768, 2048], P('ep'), may hold values from -0.21875 to 0.21875
Outputs:
- layer_out: bfloat16 [131072, 2048], P(('ep', 'dp'))
- router_grad: float32 [131072, 2], P(('ep', 'dp'))
- hidden_grad: bfloat16 [327680, 768], P(('ep', 'dp'))
- weight_grad: float32 [32, 768, 2048], P('ep', 'dp')
The draws below stay inside these ranges and needn't reach their ends.
Inputs may be any that keep to these rules, and one draw needn't show every extreme that they name: `route_ids`: A token's 2 experts differ. Among the routes of one device's tokens no expert is named more than 10 times, and some device names some expert exactly 10 times.
All inputs are finite; a program needn't handle non-finite values.
Results may differ from the reference program's by a relative error of at most 0.0049.
Values may be sent and summed in bfloat16 or wider, within the bound.
No kernel may reach another device: no remote copies, remote signals or barrier semaphores. Data moves between devices by JAX's collectives and lax.ppermute only.
A program may use at most 64 MiB of HBM per device.

```python
import math
import jax
import jax.numpy as jnp
import numpy as np
from jax import lax

D = 2048
FF = 768
ROUTES = 2
TOK_DEV = 128
EXPERTS = 32
CAP = 10
ROWS_DEV = 320
TOKENS = 131072
SLOTS = 327680
N_EP = 32
N_DP = 32


def block_levels(own_key, extent, cuts, least, largest):
    factor_of = 1.0
    for axis_at, shards_of in cuts:
        draws = jax.random.uniform(jax.random.fold_in(jax.random.fold_in(own_key, 6), axis_at), (shards_of,), jnp.float32, least / len(cuts), largest / len(cuts))
        factor_of = factor_of * jnp.repeat(jnp.exp(draws), extent[axis_at] // shards_of).reshape((-1,) + (1,) * (len(extent) - 1 - axis_at))
    return factor_of


def shared_out(key, own, number, rows, amount, top, most, skew):
    ranking = jax.random.permutation(key, amount)
    crowded, usual = portions_of(amount, rows * top, most, skew, True), portions_of(amount, rows * top, most, skew, False)
    places = jnp.arange(amount)

    def named(sizes, rotation):
        used = int((sizes > 0).sum())
        fixed = max(1, used // 4)
        shifted = fixed + (places - fixed + rotation * (used - fixed)) % max(1, amount - fixed)
        return jnp.zeros((amount,), jnp.int32).at[ranking[jnp.where(places < fixed, places, shifted)]].set(jnp.asarray(sizes, jnp.int32))

    sizes = jnp.where(number % 4 == 0, named(crowded, number // 4), named(usual, number - number // 4 - 1))
    mixed = jax.random.permutation(jax.random.fold_in(own, 3), amount)
    source_of, sink = mixed[0:amount // 2 * 2:2], mixed[1:amount // 2 * 2:2]
    room = jnp.minimum(sizes[source_of] - 1, most - sizes[sink]) // 2
    room = jnp.where((source_of == ranking[0]) | (sink == ranking[0]) | (sizes[sink] == 0), 0, jnp.maximum(room, 0))
    shifted = jax.random.randint(jax.random.fold_in(own, 4), (amount // 2,), 0, 1 << 20) % (room + 1)
    sizes = sizes.at[source_of].add(-shifted).at[sink].add(shifted)
    labels = jnp.searchsorted(jnp.cumsum(sizes), jnp.arange(rows * top), side="right").astype(jnp.int32)
    table = labels.reshape(top, rows).T
    table = table[jax.random.permutation(jax.random.fold_in(own, 1), rows)]
    rotation = jax.random.randint(jax.random.fold_in(own, 2), (rows, 1), 0, top)
    return jnp.take_along_axis(table, (jnp.arange(top)[None, :] + rotation) % top, axis=1)


def portions_of(count, total, most, skew, full):
    weights = [(1 << 20) // math.isqrt(rank ** skew) + 1 for rank in range(1, count + 1)]
    largest = most if full else min(most, max(-(-total // count), total * weights[0] // sum(weights)))
    least = 1 if total - largest >= count - 1 else 0
    holding, rest = [largest] + [least] * (count - 1), total - largest - least * (count - 1)
    while rest > 0:
        movable = [i for i in range(1, count) if holding[i] < largest] or [i for i in range(1, count) if holding[i] < most]
        mass, left = sum([weights[i] for i in movable]), rest
        for i in movable:
            addition = min(most - holding[i], max(1, left * weights[i] // mass), rest)
            holding[i] = holding[i] + addition
            rest = rest - addition
    return np.array(holding)


def gaussian(key, shape, spread, reach, pieces=(), held_as=jnp.bfloat16):
    entries = spread * jax.random.normal(key, shape, jnp.float32)
    if pieces:
        entries = entries * block_levels(key, shape, pieces, -0.22, 0.18)
    return jnp.clip(entries, -reach, reach).astype(held_as)


def setup_inputs(seed: int = 0) -> dict:
    splits = jax.random.split(jax.random.key(seed), 6)
    cotangent = gaussian(splits[0], (TOKENS, D), 1.0, 6.0, ((0, 1024),))
    route_ids_keys = jax.random.split(jax.random.fold_in(splits[1], 1), TOKENS // TOK_DEV)
    route_ids_turns = jax.random.permutation(jax.random.fold_in(splits[1], 3), TOKENS // TOK_DEV)
    route_ids = jax.vmap(lambda own, number: shared_out(jax.random.fold_in(splits[1], 2), own, number, TOK_DEV, EXPERTS, ROUTES, CAP, 2))(route_ids_keys, route_ids_turns).reshape((TOKENS, ROUTES))
    route_probs = jnp.clip(jnp.exp(math.log(0.8) - 2.7725887 * jax.random.uniform(splits[2], (TOKENS, ROUTES), jnp.float32) ** block_levels(splits[2], (TOKENS, ROUTES), ((0, 1024),), -0.2, 0.2)), 0.05, 0.8)
    expert_hidden = gaussian(splits[3], (SLOTS, FF), 1.0, 6.0, ((0, 1024),))
    down_weight = gaussian(splits[4], (EXPERTS, FF, D), FF ** -0.5, 0.21875, ((0, 32),))
    return {"cotangent": cotangent, "route_ids": route_ids, "route_probs": route_probs, "expert_hidden": expert_hidden, "down_weight": down_weight}


def slot_positions(flat_ids):
    onehot = (flat_ids[..., None] == jnp.arange(EXPERTS, dtype=jnp.int32)).astype(jnp.int32)
    earlier = jnp.cumsum(onehot, axis=-2) - onehot
    return jnp.sum(earlier * onehot, axis=-1).astype(jnp.int32)


def reference(cotangent, route_ids, route_probs, expert_hidden, down_weight):
    weight_wide = down_weight.astype(jnp.float32)
    grad_scale = (N_DP * N_EP * CAP) ** -0.5
    feature_scale = D ** -0.5

    def group_step(running, inputs):
        cot_group, expert_ids, gate_probs, hidden = inputs
        flat_ids = expert_ids.reshape(N_EP, TOK_DEV * ROUTES).astype(jnp.int32)
        slot_index = slot_positions(flat_ids)
        source_index = jnp.arange(N_EP, dtype=jnp.int32)[:, None]
        row_index = (source_index * CAP + slot_index).astype(jnp.int32)
        hidden_wide = hidden.astype(jnp.float32)
        expert_out = jnp.einsum('erf,efd->erd', hidden_wide, weight_wide).astype(jnp.bfloat16)
        picked_rows = expert_out[flat_ids, row_index].reshape(N_EP, TOK_DEV, ROUTES, D)
        picked_wide = picked_rows.astype(jnp.float32)
        layer_out = jnp.sum(gate_probs[..., None] * picked_wide, axis=2).astype(jnp.bfloat16)
        cot_wide = cot_group.astype(jnp.float32)
        router_grad = jnp.einsum('ptd,ptrd->ptr', cot_wide, picked_wide) * feature_scale
        scaled_rows = (gate_probs[..., None] * cot_wide[:, :, None, :]).astype(jnp.bfloat16)
        scaled_rows = scaled_rows.reshape(N_EP, TOK_DEV * ROUTES, D)
        slot_grads = jnp.zeros((EXPERTS, ROWS_DEV, D), jnp.bfloat16).at[flat_ids, row_index].set(scaled_rows)
        grads_wide = slot_grads.astype(jnp.float32)
        hidden_grad = jnp.einsum('erd,efd->erf', grads_wide, weight_wide).astype(jnp.bfloat16)
        partial_value = jnp.einsum('erf,erd->efd', hidden_wide, grads_wide) * grad_scale
        return running + partial_value, (layer_out, router_grad, hidden_grad)

    cot_groups = jnp.moveaxis(cotangent.reshape(N_EP, N_DP, TOK_DEV, D), 1, 0)
    id_groups = jnp.moveaxis(route_ids.reshape(N_EP, N_DP, TOK_DEV, ROUTES), 1, 0)
    prob_groups = jnp.moveaxis(route_probs.reshape(N_EP, N_DP, TOK_DEV, ROUTES), 1, 0)
    hidden_groups = jnp.moveaxis(expert_hidden.reshape(EXPERTS, N_DP, ROWS_DEV, FF), 1, 0)
    start_total = jnp.zeros((EXPERTS, FF, D), jnp.float32)
    grad_total, results = lax.scan(group_step, start_total, (cot_groups, id_groups, prob_groups, hidden_groups))
    layer_out, router_grad, hidden_grad = results
    layer_out = jnp.moveaxis(layer_out, 0, 1).reshape(TOKENS, D)
    router_grad = jnp.moveaxis(router_grad, 0, 1).reshape(TOKENS, ROUTES)
    hidden_grad = jnp.moveaxis(hidden_grad, 0, 1).reshape(SLOTS, FF)
    return layer_out, router_grad, hidden_grad, grad_total
```

```python
import jax
import jax.numpy as jnp
from jax import lax
from jax.experimental import pallas as pl
from jax.experimental.pallas import tpu as pltpu
from jax.sharding import PartitionSpec as P

BF16 = jnp.bfloat16
F32 = jnp.float32
QUARTERS = 4
VMEM_BYTES = 48 * 1024 * 1024


def iota(shape, dim):
    return lax.broadcasted_iota(jnp.int32, shape, dim)


def dot(a, b, a_dim=1, b_dim=0):
    return lax.dot_general(a, b, (((a_dim,), (b_dim,)), ((), ())), preferred_element_type=F32)


def onehot(condition):
    return condition.astype(F32).astype(BF16)


def quarter_mask(rows, columns, quarter):
    return (iota((rows, columns), 0) & 3) == quarter


def route_slots(ids):
    tokens = ids.shape[1]
    experts = iota((32, tokens), 0)
    hits = [jnp.where(experts == ids[r : r + 1, :], 1.0, 0.0) for r in range(2)]
    before = onehot(iota((tokens, tokens), 0) < iota((tokens, tokens), 1))
    earlier = dot((hits[0] + hits[1]).astype(BF16), before)
    return [jnp.sum(earlier * hit, axis=0, keepdims=True).astype(jnp.int32) for hit in hits]


def route_masks(ids):
    tokens = ids.shape[1]
    row = iota((256, tokens), 0)
    low, high = [], []
    for r, slot in enumerate(route_slots(ids)):
        expert = ids[r : r + 1, :]
        low.append((row == expert * 8 + slot) & (slot < 8))
        high.append(((row >> 2) == expert * 2 + slot - 8) & (slot >= 8))
    return low, high


def send_kernel(ids_ref, probs_ref, cot_ref, out_ref):
    low, high = route_masks(ids_ref[...])
    probs = probs_ref[...]

    def weigh(masks):
        weights = [jnp.where(mask, probs[r : r + 1, :], 0.0) for r, mask in enumerate(masks)]
        return jnp.sum(weights[0] + weights[1], axis=1, keepdims=True)

    low_select = onehot(low[0] | low[1])
    high_select = onehot(high[0] | high[1])
    low_weight, high_weight = weigh(low), weigh(high)
    width = cot_ref.shape[1] // QUARTERS
    left = jnp.zeros((256, width), F32)
    for q in range(QUARTERS):
        part = cot_ref[:, q * width : (q + 1) * width]
        out_ref[:, q * width : (q + 1) * width] = (low_weight * dot(low_select, part)).astype(BF16)
        left = jnp.where(quarter_mask(256, width, q), dot(high_select, part), left)
    out_ref[:, QUARTERS * width :] = (high_weight * left).astype(BF16)


def expert_kernel(hidden_ref, weight_ref, out_ref, packed_ref, left_ref):
    step = pl.program_id(0)
    rows = hidden_ref.shape[0]
    width = weight_ref.shape[1]

    @pl.when(step == 0)
    def _():
        row, column = iota((256, rows), 0), iota((256, rows), 1)
        peer, place = row >> 3, row & 7
        hidden = hidden_ref[...]
        packed_ref[0:256, :] = dot(onehot(column == peer * 10 + place), hidden).astype(BF16)
        packed_ref[256:512, :] = dot(onehot(column == peer * 10 + 8 + (place >> 2)), hidden).astype(BF16)
        left_ref[...] = jnp.zeros_like(left_ref)

    both = dot(packed_ref[...], weight_ref[...])
    left_ref[...] = jnp.where(quarter_mask(256, width, step), both[256:512, :], left_ref[...])
    out_ref[:, pl.ds(pl.multiple_of(step * width, width), width)] = both[0:256, :].astype(BF16)

    @pl.when(step == QUARTERS - 1)
    def _():
        out_ref[:, QUARTERS * width :] = left_ref[...].astype(BF16)


def natural_rows(low, left, step, rows):
    row, column = iota((rows, 512), 0), iota((rows, 512), 1)
    peer, place = (column & 255) >> 3, column & 7
    in_low = (column < 256) & (row == peer * 10 + place)
    in_left = (column >= 256) & (row == peer * 10 + 8 + (place >> 2)) & ((place & 3) == step)
    return dot(onehot(in_low | in_left), jnp.concatenate([low, left], axis=0)).astype(BF16)


def partial_kernel(scale, hidden_ref, low_ref, left_ref, out_ref, turned_ref):
    step = pl.program_id(0)

    @pl.when(step == 0)
    def _():
        turned_ref[...] = hidden_ref[...].T

    rows = natural_rows(low_ref[...], left_ref[...], step, hidden_ref.shape[0])
    out_ref[...] = dot(turned_ref[...], rows) * scale


def hidden_grad_kernel(low_ref, left_ref, weight_ref, out_ref, total_ref):
    step = pl.program_id(0)
    rows = natural_rows(low_ref[...], left_ref[...], step, out_ref.shape[0])
    term = dot(rows, weight_ref[...], 1, 1)

    @pl.when(step == 0)
    def _():
        total_ref[...] = term

    @pl.when(step > 0)
    def _():
        total_ref[...] += term

    @pl.when(step == QUARTERS - 1)
    def _():
        out_ref[...] = total_ref[...].astype(BF16)


def combine_kernel(ids_ref, probs_ref, cot_ref, rows_ref, out_ref, grad_ref):
    tokens, features = cot_ref.shape
    width = features // QUARTERS
    low, high = route_masks(ids_ref[...])
    diagonal = iota((tokens, tokens), 0) == iota((tokens, tokens), 1)
    probs = [
        jnp.sum(jnp.where(diagonal, probs_ref[r : r + 1, :], 0.0), axis=1, keepdims=True)
        for r in range(2)
    ]
    left = rows_ref[:, QUARTERS * width :]
    sums = [jnp.zeros((tokens, 1), F32) for _ in range(2)]
    for q in range(QUARTERS):
        part = slice(q * width, (q + 1) * width)
        held = jnp.concatenate([rows_ref[:, part], left], axis=0)
        mine = quarter_mask(256, tokens, q)
        cot = cot_ref[:, part].astype(F32)
        total = jnp.zeros((tokens, width), F32)
        for r in range(2):
            select = jnp.concatenate([onehot(low[r]), onehot(high[r] & mine)], axis=0)
            picked = dot(select, held, 0, 0)
            total += probs[r] * picked
            sums[r] += jnp.sum(cot * picked, axis=1, keepdims=True)
        out_ref[:, part] = total.astype(BF16)
    for r in range(2):
        grad_ref[r : r + 1, :] = (
            jnp.sum(jnp.where(diagonal, sums[r], 0.0), axis=0, keepdims=True) * features ** (-0.5)
        )


def call(kernel, out_shape, flops, bytes_accessed, **options):
    return pl.pallas_call(
        kernel,
        out_shape=out_shape,
        compiler_params=pltpu.CompilerParams(vmem_limit_bytes=VMEM_BYTES),
        cost_estimate=pl.CostEstimate(
            flops=flops, bytes_accessed=bytes_accessed, transcendentals=0
        ),
        **options,
    )


def exchange(packed, peers):
    blocks = packed.reshape(peers, packed.shape[0] // peers, packed.shape[1])
    return lax.all_to_all(blocks, "ep", split_axis=0, concat_axis=0, tiled=True).reshape(packed.shape)


def shards(cotangent, route_ids, route_probs, expert_hidden, down_weight):
    peers, groups = lax.axis_size("ep"), lax.axis_size("dp")
    tokens, features = cotangent.shape
    rows, inner = expert_hidden.shape
    weight = down_weight[0]
    ids, probs = route_ids.T, route_probs.T
    width = features // QUARTERS
    packed = jax.ShapeDtypeStruct((256, features + width), BF16)
    product = 2 * rows * inner * features
    whole = lambda shape: pl.BlockSpec(shape, lambda q: (0,) * len(shape))
    column = lambda height: pl.BlockSpec((height, width), lambda q: (0, q))
    last = pl.BlockSpec((256, width), lambda q: (0, QUARTERS))

    outgoing = call(send_kernel, packed, 4 * 256 * tokens * features, 2 * 10**6)(ids, probs, cotangent)
    arrived = exchange(outgoing, peers)
    expert_rows = call(
        expert_kernel,
        packed,
        2 * product,
        6 * 10**6,
        grid=(QUARTERS,),
        in_specs=[whole((rows, inner)), column(inner)],
        out_specs=whole(packed.shape),
        scratch_shapes=[pltpu.VMEM((512, inner), BF16), pltpu.VMEM((256, width), F32)],
    )(expert_hidden, weight)
    partial = call(
        lambda *refs: partial_kernel((groups * rows) ** (-0.5), *refs),
        jax.ShapeDtypeStruct((inner, features), F32),
        2 * product,
        8 * 10**6,
        grid=(QUARTERS,),
        in_specs=[whole((rows, inner)), column(256), last],
        out_specs=column(inner),
        scratch_shapes=[pltpu.VMEM((inner, rows), BF16)],
    )(expert_hidden, arrived, arrived)
    weight_grad = lax.psum_scatter(partial, "dp", scatter_dimension=0, tiled=True)
    returned = exchange(expert_rows, peers)
    hidden_grad = call(
        hidden_grad_kernel,
        jax.ShapeDtypeStruct((rows, inner), BF16),
        2 * product,
        6 * 10**6,
        grid=(QUARTERS,),
        in_specs=[column(256), last, column(inner)],
        out_specs=whole((rows, inner)),
        scratch_shapes=[pltpu.VMEM((rows, inner), F32)],
    )(arrived, arrived, weight)
    layer_out, router_grad = call(
        combine_kernel,
        (
            jax.ShapeDtypeStruct((tokens, features), BF16),
            jax.ShapeDtypeStruct((2, tokens), F32),
        ),
        8 * 256 * tokens * features,
        3 * 10**6,
    )(ids, probs, cotangent, returned)
    return (layer_out, router_grad.T, hidden_grad, weight_grad[None])


def solution(mesh):
    in_specs = (
        P(("ep", "dp"), None),
        P(("ep", "dp"), None),
        P(("ep", "dp"), None),
        P(("ep", "dp"), None),
        P("ep", None, None),
    )
    out_specs = (
        P(("ep", "dp"), None),
        P(("ep", "dp"), None),
        P(("ep", "dp"), None),
        P("ep", "dp", None),
    )
    return jax.shard_map(shards, mesh=mesh, in_specs=in_specs, out_specs=out_specs, check_vma=False)
```

```python
import jax
import jax.numpy as jnp
from jax import lax
from jax.experimental import pallas as pl
from jax.experimental.pallas import tpu as pltpu
from jax.sharding import PartitionSpec as P

BF16 = jnp.bfloat16
F32 = jnp.float32
QUARTERS = 4
CHUNK = 24
VMEM_BYTES = 48 * 1024 * 1024


def iota(shape, dim):
    return lax.broadcasted_iota(jnp.int32, shape, dim)


def dot(a, b, a_dim=1, b_dim=0):
    return lax.dot_general(a, b, (((a_dim,), (b_dim,)), ((), ())), preferred_element_type=F32)


def onehot(condition):
    return condition.astype(F32).astype(BF16)


def quarter_mask(rows, columns, quarter):
    return (iota((rows, columns), 0) & 3) == quarter


def route_slots(ids):
    tokens = ids.shape[1]
    experts = iota((32, tokens), 0)
    hits = [jnp.where(experts == ids[r : r + 1, :], 1.0, 0.0) for r in range(2)]
    before = onehot(iota((tokens, tokens), 0) < iota((tokens, tokens), 1))
    earlier = dot((hits[0] + hits[1]).astype(BF16), before)
    return [jnp.sum(earlier * hit, axis=0, keepdims=True).astype(jnp.int32) for hit in hits]


def route_masks(ids):
    tokens = ids.shape[1]
    row = iota((256, tokens), 0)
    low, high = [], []
    for r, slot in enumerate(route_slots(ids)):
        expert = ids[r : r + 1, :]
        low.append((row == expert * 8 + slot) & (slot < 8))
        high.append(((row >> 2) == expert * 2 + slot - 8) & (slot >= 8))
    return low, high


def send_kernel(ids_ref, probs_ref, cot_ref, out_ref):
    low, high = route_masks(ids_ref[...])
    probs = probs_ref[...]

    def weigh(masks):
        weights = [jnp.where(mask, probs[r : r + 1, :], 0.0) for r, mask in enumerate(masks)]
        return jnp.sum(weights[0] + weights[1], axis=1, keepdims=True)

    low_select = onehot(low[0] | low[1])
    high_select = onehot(high[0] | high[1])
    low_weight, high_weight = weigh(low), weigh(high)
    width = cot_ref.shape[1] // QUARTERS
    left = jnp.zeros((256, width), F32)
    for q in range(QUARTERS):
        part = cot_ref[:, q * width : (q + 1) * width]
        out_ref[:, q * width : (q + 1) * width] = (low_weight * dot(low_select, part)).astype(BF16)
        left = jnp.where(quarter_mask(256, width, q), dot(high_select, part), left)
    out_ref[:, QUARTERS * width :] = (high_weight * left).astype(BF16)


def expert_kernel(hidden_ref, weight_ref, out_ref, packed_ref, left_ref):
    step = pl.program_id(0)
    rows = hidden_ref.shape[0]
    width = weight_ref.shape[1]

    @pl.when(step == 0)
    def _():
        row, column = iota((256, rows), 0), iota((256, rows), 1)
        peer, place = row >> 3, row & 7
        hidden = hidden_ref[...]
        packed_ref[0:256, :] = dot(onehot(column == peer * 10 + place), hidden).astype(BF16)
        packed_ref[256:512, :] = dot(onehot(column == peer * 10 + 8 + (place >> 2)), hidden).astype(BF16)
        left_ref[...] = jnp.zeros_like(left_ref)

    both = dot(packed_ref[...], weight_ref[...])
    left_ref[...] = jnp.where(quarter_mask(256, width, step), both[256:512, :], left_ref[...])
    out_ref[:, pl.ds(pl.multiple_of(step * width, width), width)] = both[0:256, :].astype(BF16)

    @pl.when(step == QUARTERS - 1)
    def _():
        out_ref[:, QUARTERS * width :] = left_ref[...].astype(BF16)


def natural_rows(low, left, step, rows):
    row, column = iota((rows, 512), 0), iota((rows, 512), 1)
    peer, place = (column & 255) >> 3, column & 7
    in_low = (column < 256) & (row == peer * 10 + place)
    in_left = (column >= 256) & (row == peer * 10 + 8 + (place >> 2)) & ((place & 3) == step)
    return dot(onehot(in_low | in_left), jnp.concatenate([low, left], axis=0)).astype(BF16)


def chunk_order(group, rows):
    block = (rows * 2731) >> 16
    offset = jnp.where(block < 11, 14 - 3 * block, jnp.where(block < 21, 46 - 3 * block, 78 - 3 * block))
    return ((group + offset) & 31) * CHUNK + rows - block * CHUNK


def partial_kernel(scale, group_ref, hidden_ref, low_ref, left_ref, down_ref, up_ref, own_ref, turned_ref):
    step = pl.program_id(0)
    inner = hidden_ref.shape[1]

    @pl.when(step == 0)
    def _():
        source = chunk_order(group_ref[0], iota((1, inner), 1))
        select = onehot(iota((inner, inner), 0) == source)
        turned_ref[...] = dot(select, hidden_ref[...], 0, 1).astype(BF16)

    rows = natural_rows(low_ref[...], left_ref[...], step, hidden_ref.shape[0])
    product = dot(turned_ref[...], rows) * scale
    down_ref[...] = product[: 11 * CHUNK].astype(BF16)
    up_ref[...] = product[11 * CHUNK : 21 * CHUNK].astype(BF16)
    own_ref[...] = product[21 * CHUNK :]


def shift(block, distance):
    groups = lax.axis_size("dp")
    return lax.ppermute(block, "dp", [(i, (i + distance) % groups) for i in range(groups)])


def sum_over_groups(from_above, from_below, own):
    def term(k):
        place = slice(k * CHUNK, (k + 1) * CHUNK)
        total = own[place] + from_above[place].astype(F32)
        return total if k == 0 else total + from_below[(k - 1) * CHUNK : k * CHUNK].astype(F32)

    rising, falling = term(0), term(10)
    for k in range(1, 5):
        rising = shift(rising.astype(BF16), 3).astype(F32) + term(k)
        falling = shift(falling.astype(BF16), -3).astype(F32) + term(10 - k)
    rising, falling = shift(rising.astype(BF16), 3), shift(falling.astype(BF16), -3)
    return term(5) + rising.astype(F32) + falling.astype(F32)


def hidden_grad_kernel(low_ref, left_ref, weight_ref, out_ref, total_ref):
    step = pl.program_id(0)
    rows = natural_rows(low_ref[...], left_ref[...], step, out_ref.shape[0])
    term = dot(rows, weight_ref[...], 1, 1)

    @pl.when(step == 0)
    def _():
        total_ref[...] = term

    @pl.when(step > 0)
    def _():
        total_ref[...] += term

    @pl.when(step == QUARTERS - 1)
    def _():
        out_ref[...] = total_ref[...].astype(BF16)


def combine_kernel(ids_ref, probs_ref, cot_ref, rows_ref, out_ref, grad_ref):
    tokens, features = cot_ref.shape
    width = features // QUARTERS
    low, high = route_masks(ids_ref[...])
    diagonal = iota((tokens, tokens), 0) == iota((tokens, tokens), 1)
    probs = [
        jnp.sum(jnp.where(diagonal, probs_ref[r : r + 1, :], 0.0), axis=1, keepdims=True)
        for r in range(2)
    ]
    left = rows_ref[:, QUARTERS * width :]
    sums = [jnp.zeros((tokens, 1), F32) for _ in range(2)]
    for q in range(QUARTERS):
        part = slice(q * width, (q + 1) * width)
        held = jnp.concatenate([rows_ref[:, part], left], axis=0)
        mine = quarter_mask(256, tokens, q)
        cot = cot_ref[:, part].astype(F32)
        total = jnp.zeros((tokens, width), F32)
        for r in range(2):
            select = jnp.concatenate([onehot(low[r]), onehot(high[r] & mine)], axis=0)
            picked = dot(select, held, 0, 0)
            total += probs[r] * picked
            sums[r] += jnp.sum(cot * picked, axis=1, keepdims=True)
        out_ref[:, part] = total.astype(BF16)
    for r in range(2):
        grad_ref[r : r + 1, :] = (
            jnp.sum(jnp.where(diagonal, sums[r], 0.0), axis=0, keepdims=True) * features ** (-0.5)
        )


def call(kernel, out_shape, flops, bytes_accessed, **options):
    return pl.pallas_call(
        kernel,
        out_shape=out_shape,
        compiler_params=pltpu.CompilerParams(vmem_limit_bytes=VMEM_BYTES),
        cost_estimate=pl.CostEstimate(
            flops=flops, bytes_accessed=bytes_accessed, transcendentals=0
        ),
        **options,
    )


def exchange(packed, peers):
    blocks = packed.reshape(peers, packed.shape[0] // peers, packed.shape[1])
    return lax.all_to_all(blocks, "ep", split_axis=0, concat_axis=0, tiled=True).reshape(packed.shape)


def shards(cotangent, route_ids, route_probs, expert_hidden, down_weight):
    peers, groups = lax.axis_size("ep"), lax.axis_size("dp")
    tokens, features = cotangent.shape
    rows, inner = expert_hidden.shape
    weight = down_weight[0]
    ids, probs = route_ids.T, route_probs.T
    width = features // QUARTERS
    packed = jax.ShapeDtypeStruct((256, features + width), BF16)
    product = 2 * rows * inner * features
    whole = lambda shape: pl.BlockSpec(shape, lambda q: (0,) * len(shape))
    column = lambda height: pl.BlockSpec((height, width), lambda q: (0, q))
    last = pl.BlockSpec((256, width), lambda q: (0, QUARTERS))

    outgoing = call(send_kernel, packed, 4 * 256 * tokens * features, 2 * 10**6)(ids, probs, cotangent)
    arrived = exchange(outgoing, peers)
    expert_rows = call(
        expert_kernel,
        packed,
        2 * product,
        6 * 10**6,
        grid=(QUARTERS,),
        in_specs=[whole((rows, inner)), column(inner)],
        out_specs=whole(packed.shape),
        scratch_shapes=[pltpu.VMEM((512, inner), BF16), pltpu.VMEM((256, width), F32)],
    )(expert_hidden, weight)
    group = lax.axis_index("dp").astype(jnp.int32).reshape(1)
    down, up, own = call(
        lambda *refs: partial_kernel((groups * rows) ** (-0.5), *refs),
        (
            jax.ShapeDtypeStruct((11 * CHUNK, features), BF16),
            jax.ShapeDtypeStruct((10 * CHUNK, features), BF16),
            jax.ShapeDtypeStruct((11 * CHUNK, features), F32),
        ),
        2 * product,
        8 * 10**6,
        grid=(QUARTERS,),
        in_specs=[
            pl.BlockSpec(memory_space=pltpu.SMEM),
            whole((rows, inner)),
            column(256),
            last,
        ],
        out_specs=(column(11 * CHUNK), column(10 * CHUNK), column(11 * CHUNK)),
        scratch_shapes=[pltpu.VMEM((inner, rows), BF16)],
    )(group, expert_hidden, arrived, arrived)
    expert_rows, down, up = lax.optimization_barrier((expert_rows, down, up))
    from_above, from_below = shift(down, -1), shift(up, 1)
    returned = exchange(expert_rows, peers)
    returned, from_above, from_below = lax.optimization_barrier((returned, from_above, from_below))
    weight_grad = sum_over_groups(from_above, from_below, own)
    hidden_grad = call(
        hidden_grad_kernel,
        jax.ShapeDtypeStruct((rows, inner), BF16),
        2 * product,
        6 * 10**6,
        grid=(QUARTERS,),
        in_specs=[column(256), last, column(inner)],
        out_specs=whole((rows, inner)),
        scratch_shapes=[pltpu.VMEM((rows, inner), F32)],
    )(arrived, arrived, weight)
    layer_out, router_grad = call(
        combine_kernel,
        (
            jax.ShapeDtypeStruct((tokens, features), BF16),
            jax.ShapeDtypeStruct((2, tokens), F32),
        ),
        8 * 256 * tokens * features,
        3 * 10**6,
    )(ids, probs, cotangent, returned)
    return (layer_out, router_grad.T, hidden_grad, weight_grad[None])


def solution(mesh):
    in_specs = (
        P(("ep", "dp"), None),
        P(("ep", "dp"), None),
        P(("ep", "dp"), None),
        P(("ep", "dp"), None),
        P("ep", None, None),
    )
    out_specs = (
        P(("ep", "dp"), None),
        P(("ep", "dp"), None),
        P(("ep", "dp"), None),
        P("ep", "dp", None),
    )
    return jax.shard_map(shards, mesh=mesh, in_specs=in_specs, out_specs=out_specs, check_vma=False)
```

```python
import jax
import jax.numpy as jnp
from jax import lax
from jax.experimental import pallas as pl
from jax.experimental.pallas import tpu as pltpu
from jax.sharding import PartitionSpec as P

BF16 = jnp.bfloat16
F32 = jnp.float32
QUARTERS = 4
HALVES = 2
CHUNK = 24
VMEM_BYTES = 48 * 1024 * 1024


def iota(shape, dim):
    return lax.broadcasted_iota(jnp.int32, shape, dim)


def dot(a, b, a_dim=1, b_dim=0):
    return lax.dot_general(a, b, (((a_dim,), (b_dim,)), ((), ())), preferred_element_type=F32)


def onehot(condition):
    return condition.astype(F32).astype(BF16)


def quarter_mask(rows, columns, quarter):
    return (iota((rows, columns), 0) & 3) == quarter


def route_slots(ids):
    tokens = ids.shape[1]
    experts = iota((32, tokens), 0)
    hits = [jnp.where(experts == ids[r : r + 1, :], 1.0, 0.0) for r in range(2)]
    before = onehot(iota((tokens, tokens), 0) < iota((tokens, tokens), 1))
    earlier = dot((hits[0] + hits[1]).astype(BF16), before)
    return [jnp.sum(earlier * hit, axis=0, keepdims=True).astype(jnp.int32) for hit in hits]


def route_masks(ids):
    tokens = ids.shape[1]
    row = iota((256, tokens), 0)
    low, high = [], []
    for r, slot in enumerate(route_slots(ids)):
        expert = ids[r : r + 1, :]
        low.append((row == expert * 8 + slot) & (slot < 8))
        high.append(((row >> 2) == expert * 2 + slot - 8) & (slot >= 8))
    return low, high


def send_kernel(ids_ref, probs_ref, cot_ref, *out_refs):
    low, high = route_masks(ids_ref[...])
    probs = probs_ref[...]

    def weigh(masks):
        weights = [jnp.where(mask, probs[r : r + 1, :], 0.0) for r, mask in enumerate(masks)]
        return jnp.sum(weights[0] + weights[1], axis=1, keepdims=True)

    low_select = onehot(low[0] | low[1])
    high_select = onehot(high[0] | high[1])
    low_weight, high_weight = weigh(low), weigh(high)
    width = cot_ref.shape[1] // (HALVES * QUARTERS)
    for h, out_ref in enumerate(out_refs):
        left = jnp.zeros((256, width), F32)
        for q in range(QUARTERS):
            start = (h * QUARTERS + q) * width
            part = cot_ref[:, start : start + width]
            rows = low_weight * dot(low_select, part)
            out_ref[:, q * width : (q + 1) * width] = rows.astype(BF16)
            left = jnp.where(quarter_mask(256, width, q), dot(high_select, part), left)
        out_ref[:, QUARTERS * width :] = (high_weight * left).astype(BF16)


def expert_kernel(hidden_ref, weight_ref, out_ref, packed_ref, left_ref):
    step = pl.program_id(0)
    rows = hidden_ref.shape[0]
    width = weight_ref.shape[1]

    @pl.when(step == 0)
    def _():
        row, column = iota((256, rows), 0), iota((256, rows), 1)
        peer, place = row >> 3, row & 7
        hidden = hidden_ref[...]
        packed_ref[0:256, :] = dot(onehot(column == peer * 10 + place), hidden).astype(BF16)
        packed_ref[256:512, :] = dot(onehot(column == peer * 10 + 8 + (place >> 2)), hidden).astype(BF16)
        left_ref[...] = jnp.zeros_like(left_ref)

    both = dot(packed_ref[...], weight_ref[...])
    left_ref[...] = jnp.where(quarter_mask(256, width, step), both[256:512, :], left_ref[...])
    out_ref[:, pl.ds(pl.multiple_of(step * width, width), width)] = both[0:256, :].astype(BF16)

    @pl.when(step == QUARTERS - 1)
    def _():
        out_ref[:, QUARTERS * width :] = left_ref[...].astype(BF16)


def natural_rows(low, left, step, rows):
    row, column = iota((rows, 512), 0), iota((rows, 512), 1)
    peer, place = (column & 255) >> 3, column & 7
    in_low = (column < 256) & (row == peer * 10 + place)
    in_left = (column >= 256) & (row == peer * 10 + 8 + (place >> 2)) & ((place & 3) == step)
    return dot(onehot(in_low | in_left), jnp.concatenate([low, left], axis=0)).astype(BF16)


def chunk_order(group, rows):
    block = (rows * 2731) >> 16
    offset = jnp.where(block < 11, 14 - 3 * block, jnp.where(block < 21, 46 - 3 * block, 78 - 3 * block))
    return ((group + offset) & 31) * CHUNK + rows - block * CHUNK


def turn_kernel(group_ref, hidden_ref, turned_ref):
    inner = hidden_ref.shape[1]
    source = chunk_order(group_ref[0], iota((1, inner), 1))
    select = onehot(iota((inner, inner), 0) == source)
    turned_ref[...] = dot(select, hidden_ref[...], 0, 1).astype(BF16)


def partial_kernel(scale, turned_ref, low_ref, left_ref, down_ref, up_ref, own_ref):
    rows = natural_rows(low_ref[...], left_ref[...], pl.program_id(0), turned_ref.shape[1])
    product = dot(turned_ref[...], rows) * scale
    down_ref[...] = product[: 11 * CHUNK].astype(BF16)
    up_ref[...] = product[11 * CHUNK : 21 * CHUNK].astype(BF16)
    own_ref[...] = product[21 * CHUNK :]


def shift(block, distance):
    groups = lax.axis_size("dp")
    return lax.ppermute(block, "dp", [(i, (i + distance) % groups) for i in range(groups)])


def sum_over_groups(halves, expert_rows, combine):
    def term(k):
        parts = []
        for from_above, from_below, own in halves:
            place = slice(k * CHUNK, (k + 1) * CHUNK)
            total = own[place] + from_above[place].astype(F32)
            if k > 0:
                total += from_below[(k - 1) * CHUNK : k * CHUNK].astype(F32)
            parts.append(total)
        return jnp.concatenate(parts, axis=1)

    rising, falling = term(0), term(10)
    for k in range(1, 5):
        rising, falling = shift(rising.astype(BF16), 3), shift(falling.astype(BF16), -3)
        if k == 1:
            rising, expert_rows = lax.optimization_barrier((rising, expert_rows))
            combined = combine(expert_rows)
        if k == 4:
            rising, falling, combined = lax.optimization_barrier((rising, falling, combined))
        rising, falling = rising.astype(F32) + term(k), falling.astype(F32) + term(10 - k)
    rising, falling = shift(rising.astype(BF16), 3), shift(falling.astype(BF16), -3)
    return term(5) + rising.astype(F32) + falling.astype(F32), combined


def hidden_grad_kernel(*refs):
    inputs, (out_ref, total_ref) = refs[:-2], refs[-2:]
    step = pl.program_id(0)
    term = 0.0
    for low_ref, left_ref, weight_ref in zip(inputs[0::3], inputs[1::3], inputs[2::3]):
        rows = natural_rows(low_ref[...], left_ref[...], step, out_ref.shape[0])
        term += dot(rows, weight_ref[...], 1, 1)

    @pl.when(step == 0)
    def _():
        total_ref[...] = term

    @pl.when(step > 0)
    def _():
        total_ref[...] += term

    @pl.when(step == QUARTERS - 1)
    def _():
        out_ref[...] = total_ref[...].astype(BF16)


def combine_kernel(ids_ref, probs_ref, cot_ref, rows_ref, out_ref, grad_ref):
    tokens, features = cot_ref.shape
    width = features // QUARTERS
    low, high = route_masks(ids_ref[...])
    diagonal = iota((tokens, tokens), 0) == iota((tokens, tokens), 1)
    probs = [
        jnp.sum(jnp.where(diagonal, probs_ref[r : r + 1, :], 0.0), axis=1, keepdims=True)
        for r in range(2)
    ]
    left = rows_ref[:, QUARTERS * width :]
    sums = [jnp.zeros((tokens, 1), F32) for _ in range(2)]
    for q in range(QUARTERS):
        part = slice(q * width, (q + 1) * width)
        held = jnp.concatenate([rows_ref[:, part], left], axis=0)
        mine = quarter_mask(256, tokens, q)
        cot = cot_ref[:, part].astype(F32)
        total = jnp.zeros((tokens, width), F32)
        for r in range(2):
            select = jnp.concatenate([onehot(low[r]), onehot(high[r] & mine)], axis=0)
            picked = dot(select, held, 0, 0)
            total += probs[r] * picked
            sums[r] += jnp.sum(cot * picked, axis=1, keepdims=True)
        out_ref[:, part] = total.astype(BF16)
    for r in range(2):
        grad_ref[r : r + 1, :] = (
            jnp.sum(jnp.where(diagonal, sums[r], 0.0), axis=0, keepdims=True) * features ** (-0.5)
        )


def call(kernel, out_shape, flops, bytes_accessed, **options):
    return pl.pallas_call(
        kernel,
        out_shape=out_shape,
        compiler_params=pltpu.CompilerParams(vmem_limit_bytes=VMEM_BYTES),
        cost_estimate=pl.CostEstimate(
            flops=flops, bytes_accessed=bytes_accessed, transcendentals=0
        ),
        **options,
    )


def exchange(packed, peers):
    blocks = packed.reshape(peers, packed.shape[0] // peers, packed.shape[1])
    return lax.all_to_all(blocks, "ep", split_axis=0, concat_axis=0, tiled=True).reshape(packed.shape)


def shards(cotangent, route_ids, route_probs, expert_hidden, down_weight):
    peers, groups = lax.axis_size("ep"), lax.axis_size("dp")
    tokens, features = cotangent.shape
    rows, inner = expert_hidden.shape
    weight = down_weight[0]
    ids, probs = route_ids.T, route_probs.T
    width = features // QUARTERS
    packed = jax.ShapeDtypeStruct((256, features + width), BF16)
    product = 2 * rows * inner * features
    whole = lambda shape: pl.BlockSpec(shape, lambda q: (0,) * len(shape))
    column = lambda height: pl.BlockSpec((height, width), lambda q: (0, q))

    half = features // HALVES
    narrow = half // QUARTERS
    half_packed = jax.ShapeDtypeStruct((256, half + narrow), BF16)
    block = lambda height, at: pl.BlockSpec((height, narrow), lambda q: (0, at(q)))
    half_low, half_left = block(256, lambda q: q), block(256, lambda q: QUARTERS)
    outgoing = call(send_kernel, (half_packed,) * HALVES, 4 * 256 * tokens * features, 2 * 10**6)(
        ids, probs, cotangent
    )
    group = lax.axis_index("dp").astype(jnp.int32).reshape(1)
    turned = call(
        turn_kernel,
        jax.ShapeDtypeStruct((inner, rows), BF16),
        2 * inner * inner * rows,
        10**6,
        in_specs=[pl.BlockSpec(memory_space=pltpu.SMEM), pl.BlockSpec(memory_space=pltpu.VMEM)],
    )(group, expert_hidden)
    expert_rows = call(
        expert_kernel,
        packed,
        2 * product,
        6 * 10**6,
        grid=(QUARTERS,),
        in_specs=[whole((rows, inner)), column(inner)],
        out_specs=whole(packed.shape),
        scratch_shapes=[pltpu.VMEM((512, inner), BF16), pltpu.VMEM((256, width), F32)],
    )(expert_hidden, weight)

    def partial(arrived):
        return call(
            lambda *refs: partial_kernel((groups * rows) ** (-0.5), *refs),
            (
                jax.ShapeDtypeStruct((11 * CHUNK, half), BF16),
                jax.ShapeDtypeStruct((10 * CHUNK, half), BF16),
                jax.ShapeDtypeStruct((11 * CHUNK, half), F32),
            ),
            product,
            4 * 10**6,
            grid=(QUARTERS,),
            in_specs=[whole((inner, rows)), half_low, half_left],
            out_specs=tuple(block(n * CHUNK, lambda q: q) for n in (11, 10, 11)),
        )(turned, arrived, arrived)

    first = exchange(outgoing[0], peers)
    first, behind = lax.optimization_barrier((first, outgoing[1]))
    second = exchange(behind, peers)
    down_0, up_0, own_0 = partial(first)
    above_0, below_0 = shift(down_0, -1), shift(up_0, 1)
    down_1, up_1, own_1 = partial(second)
    above_1, below_1 = shift(down_1, -1), shift(up_1, 1)
    hidden_grad = call(
        hidden_grad_kernel,
        jax.ShapeDtypeStruct((rows, inner), BF16),
        2 * product,
        6 * 10**6,
        grid=(QUARTERS,),
        in_specs=[half_low, half_left, block(inner, lambda q: q)]
        + [half_low, half_left, block(inner, lambda q: QUARTERS + q)],
        out_specs=whole((rows, inner)),
        scratch_shapes=[pltpu.VMEM((rows, inner), F32)],
    )(first, first, weight, second, second, weight)
    above_1, below_1, hidden_grad = lax.optimization_barrier((above_1, below_1, hidden_grad))

    def combine(packed_rows):
        return call(
            combine_kernel,
            (
                jax.ShapeDtypeStruct((tokens, features), BF16),
                jax.ShapeDtypeStruct((2, tokens), F32),
            ),
            8 * 256 * tokens * features,
            3 * 10**6,
        )(ids, probs, cotangent, exchange(packed_rows, peers))

    weight_grad, (layer_out, router_grad) = sum_over_groups(
        ((above_0, below_0, own_0), (above_1, below_1, own_1)), expert_rows, combine
    )
    return (layer_out, router_grad.T, hidden_grad, weight_grad[None])


def solution(mesh):
    in_specs = (
        P(("ep", "dp"), None),
        P(("ep", "dp"), None),
        P(("ep", "dp"), None),
        P(("ep", "dp"), None),
        P("ep", None, None),
    )
    out_specs = (
        P(("ep", "dp"), None),
        P(("ep", "dp"), None),
        P(("ep", "dp"), None),
        P("ep", "dp", None),
    )
    return jax.shard_map(shards, mesh=mesh, in_specs=in_specs, out_specs=out_specs, check_vma=False)
```

```python
import jax
import jax.numpy as jnp
from jax import lax
from jax.experimental import pallas as pl
from jax.experimental.pallas import tpu as pltpu
from jax.sharding import PartitionSpec as P

BF16 = jnp.bfloat16
F32 = jnp.float32
QUARTERS = 4
HALVES = 2
CHUNK = 24
VMEM_BYTES = 48 * 1024 * 1024


def iota(shape, dim):
    return lax.broadcasted_iota(jnp.int32, shape, dim)


def dot(a, b, a_dim=1, b_dim=0):
    return lax.dot_general(a, b, (((a_dim,), (b_dim,)), ((), ())), preferred_element_type=F32)


def onehot(condition):
    return condition.astype(F32).astype(BF16)


def quarter_mask(rows, columns, quarter):
    return (iota((rows, columns), 0) & 3) == quarter


def route_slots(ids):
    tokens = ids.shape[1]
    experts = iota((32, tokens), 0)
    hits = [jnp.where(experts == ids[r : r + 1, :], 1.0, 0.0) for r in range(2)]
    before = onehot(iota((tokens, tokens), 0) < iota((tokens, tokens), 1))
    earlier = dot((hits[0] + hits[1]).astype(BF16), before)
    return [jnp.sum(earlier * hit, axis=0, keepdims=True).astype(jnp.int32) for hit in hits]


def route_masks(ids):
    tokens = ids.shape[1]
    row = iota((256, tokens), 0)
    low, high = [], []
    for r, slot in enumerate(route_slots(ids)):
        expert = ids[r : r + 1, :]
        low.append((row == expert * 8 + slot) & (slot < 8))
        high.append(((row >> 2) == expert * 2 + slot - 8) & (slot >= 8))
    return low, high


def send_kernel(ids_ref, probs_ref, cot_ref, *out_refs):
    low, high = route_masks(ids_ref[...])
    probs = probs_ref[...]

    def weigh(masks):
        weights = [jnp.where(mask, probs[r : r + 1, :], 0.0) for r, mask in enumerate(masks)]
        return jnp.sum(weights[0] + weights[1], axis=1, keepdims=True)

    low_select = onehot(low[0] | low[1])
    high_select = onehot(high[0] | high[1])
    low_weight, high_weight = weigh(low), weigh(high)
    width = cot_ref.shape[1] // (HALVES * QUARTERS)
    for h, out_ref in enumerate(out_refs):
        left = jnp.zeros((256, width), F32)
        for q in range(QUARTERS):
            start = (h * QUARTERS + q) * width
            part = cot_ref[:, start : start + width]
            rows = low_weight * dot(low_select, part)
            out_ref[:, q * width : (q + 1) * width] = rows.astype(BF16)
            left = jnp.where(quarter_mask(256, width, q), dot(high_select, part), left)
        out_ref[:, QUARTERS * width :] = (high_weight * left).astype(BF16)


def expert_kernel(hidden_ref, weight_ref, out_ref, packed_ref, left_ref):
    step = pl.program_id(0)
    rows = hidden_ref.shape[0]
    width = weight_ref.shape[1]

    @pl.when(step == 0)
    def _():
        row, column = iota((256, rows), 0), iota((256, rows), 1)
        peer, place = row >> 3, row & 7
        hidden = hidden_ref[...]
        packed_ref[0:256, :] = dot(onehot(column == peer * 10 + place), hidden).astype(BF16)
        packed_ref[256:512, :] = dot(onehot(column == peer * 10 + 8 + (place >> 2)), hidden).astype(BF16)
        left_ref[...] = jnp.zeros_like(left_ref)

    both = dot(packed_ref[...], weight_ref[...])
    left_ref[...] = jnp.where(quarter_mask(256, width, step), both[256:512, :], left_ref[...])
    out_ref[:, pl.ds(pl.multiple_of(step * width, width), width)] = both[0:256, :].astype(BF16)

    @pl.when(step == QUARTERS - 1)
    def _():
        out_ref[:, QUARTERS * width :] = left_ref[...].astype(BF16)


def natural_rows(low, left, step, rows):
    row, column = iota((rows, 512), 0), iota((rows, 512), 1)
    peer, place = (column & 255) >> 3, column & 7
    in_low = (column < 256) & (row == peer * 10 + place)
    in_left = (column >= 256) & (row == peer * 10 + 8 + (place >> 2)) & ((place & 3) == step)
    return dot(onehot(in_low | in_left), jnp.concatenate([low, left], axis=0)).astype(BF16)


def chunk_order(group, sign, rows):
    block = (rows * 2731) >> 16
    offset = jnp.where(block < 11, 14 - 3 * block, jnp.where(block < 21, 46 - 3 * block, 78 - 3 * block))
    return ((group + sign * offset) & 31) * CHUNK + rows - block * CHUNK


def turn_kernel(place_ref, hidden_ref, turned_ref):
    inner = hidden_ref.shape[1]
    source = chunk_order(place_ref[0], place_ref[1], iota((1, inner), 1))
    select = onehot(iota((inner, inner), 0) == source)
    turned_ref[...] = dot(select, hidden_ref[...], 0, 1).astype(BF16)


def partial_kernel(scale, turned_ref, low_ref, left_ref, down_ref, up_ref, own_ref):
    rows = natural_rows(low_ref[...], left_ref[...], pl.program_id(0), turned_ref.shape[1])
    product = dot(turned_ref[...], rows) * scale
    down_ref[...] = product[: 11 * CHUNK].astype(BF16)
    up_ref[...] = product[11 * CHUNK : 21 * CHUNK].astype(BF16)
    own_ref[...] = product[21 * CHUNK :]


def shift(block, distance):
    peers, groups = lax.axis_size("ep"), lax.axis_size("dp")
    pairs = [
        (e * groups + i, e * groups + (i + (distance if e % 2 == 0 else -distance)) % groups)
        for e in range(peers)
        for i in range(groups)
    ]
    return lax.ppermute(block, ("ep", "dp"), pairs)


def sum_over_groups(halves, returned, combine):
    def term(k):
        parts = []
        for from_above, from_below, own in halves:
            place = slice(k * CHUNK, (k + 1) * CHUNK)
            total = own[place] + from_above[place].astype(F32)
            if k > 0:
                total += from_below[(k - 1) * CHUNK : k * CHUNK].astype(F32)
            parts.append(total)
        return jnp.concatenate(parts, axis=1)

    rising, falling = term(0), term(10)
    for k in range(1, 5):
        rising, falling = shift(rising.astype(BF16), 3), shift(falling.astype(BF16), -3)
        if k == 4:
            rising, falling, combined = lax.optimization_barrier((rising, falling, combine(returned)))
        rising, falling = rising.astype(F32) + term(k), falling.astype(F32) + term(10 - k)
    rising, falling = shift(rising.astype(BF16), 3), shift(falling.astype(BF16), -3)
    return term(5) + rising.astype(F32) + falling.astype(F32), combined


def hidden_grad_kernel(*refs):
    inputs, (out_ref, total_ref) = refs[:-2], refs[-2:]
    step = pl.program_id(0)
    term = 0.0
    for low_ref, left_ref, weight_ref in zip(inputs[0::3], inputs[1::3], inputs[2::3]):
        rows = natural_rows(low_ref[...], left_ref[...], step, out_ref.shape[0])
        term += dot(rows, weight_ref[...], 1, 1)

    @pl.when(step == 0)
    def _():
        total_ref[...] = term

    @pl.when(step > 0)
    def _():
        total_ref[...] += term

    @pl.when(step == QUARTERS - 1)
    def _():
        out_ref[...] = total_ref[...].astype(BF16)


def combine_kernel(ids_ref, probs_ref, cot_ref, rows_ref, out_ref, grad_ref):
    tokens, features = cot_ref.shape
    width = features // QUARTERS
    low, high = route_masks(ids_ref[...])
    diagonal = iota((tokens, tokens), 0) == iota((tokens, tokens), 1)
    probs = [
        jnp.sum(jnp.where(diagonal, probs_ref[r : r + 1, :], 0.0), axis=1, keepdims=True)
        for r in range(2)
    ]
    left = rows_ref[:, QUARTERS * width :]
    sums = [jnp.zeros((tokens, 1), F32) for _ in range(2)]
    for q in range(QUARTERS):
        part = slice(q * width, (q + 1) * width)
        held = jnp.concatenate([rows_ref[:, part], left], axis=0)
        mine = quarter_mask(256, tokens, q)
        cot = cot_ref[:, part].astype(F32)
        total = jnp.zeros((tokens, width), F32)
        for r in range(2):
            select = jnp.concatenate([onehot(low[r]), onehot(high[r] & mine)], axis=0)
            picked = dot(select, held, 0, 0)
            total += probs[r] * picked
            sums[r] += jnp.sum(cot * picked, axis=1, keepdims=True)
        out_ref[:, part] = total.astype(BF16)
    for r in range(2):
        grad_ref[r : r + 1, :] = (
            jnp.sum(jnp.where(diagonal, sums[r], 0.0), axis=0, keepdims=True) * features ** (-0.5)
        )


def call(kernel, out_shape, flops, bytes_accessed, **options):
    return pl.pallas_call(
        kernel,
        out_shape=out_shape,
        compiler_params=pltpu.CompilerParams(vmem_limit_bytes=VMEM_BYTES),
        cost_estimate=pl.CostEstimate(
            flops=flops, bytes_accessed=bytes_accessed, transcendentals=0
        ),
        **options,
    )


def exchange(packed, peers):
    blocks = packed.reshape(peers, packed.shape[0] // peers, packed.shape[1])
    return lax.all_to_all(blocks, "ep", split_axis=0, concat_axis=0, tiled=True).reshape(packed.shape)


def shards(cotangent, route_ids, route_probs, expert_hidden, down_weight):
    peers, groups = lax.axis_size("ep"), lax.axis_size("dp")
    tokens, features = cotangent.shape
    rows, inner = expert_hidden.shape
    weight = down_weight[0]
    ids, probs = route_ids.T, route_probs.T
    width = features // QUARTERS
    packed = jax.ShapeDtypeStruct((256, features + width), BF16)
    product = 2 * rows * inner * features
    whole = lambda shape: pl.BlockSpec(shape, lambda q: (0,) * len(shape))
    column = lambda height: pl.BlockSpec((height, width), lambda q: (0, q))

    half = features // HALVES
    narrow = half // QUARTERS
    half_packed = jax.ShapeDtypeStruct((256, half + narrow), BF16)
    block = lambda height, at: pl.BlockSpec((height, narrow), lambda q: (0, at(q)))
    half_low, half_left = block(256, lambda q: q), block(256, lambda q: QUARTERS)
    outgoing = call(send_kernel, (half_packed,) * HALVES, 4 * 256 * tokens * features, 2 * 10**6)(
        ids, probs, cotangent
    )
    sign = 1 - 2 * (lax.axis_index("ep") & 1)
    place = jnp.stack([lax.axis_index("dp"), sign]).astype(jnp.int32)
    turned = call(
        turn_kernel,
        jax.ShapeDtypeStruct((inner, rows), BF16),
        2 * inner * inner * rows,
        10**6,
        in_specs=[pl.BlockSpec(memory_space=pltpu.SMEM), pl.BlockSpec(memory_space=pltpu.VMEM)],
    )(place, expert_hidden)
    expert_rows = call(
        expert_kernel,
        packed,
        2 * product,
        6 * 10**6,
        grid=(QUARTERS,),
        in_specs=[whole((rows, inner)), column(inner)],
        out_specs=whole(packed.shape),
        scratch_shapes=[pltpu.VMEM((512, inner), BF16), pltpu.VMEM((256, width), F32)],
    )(expert_hidden, weight)

    def partial(arrived):
        return call(
            lambda *refs: partial_kernel((groups * rows) ** (-0.5), *refs),
            (
                jax.ShapeDtypeStruct((11 * CHUNK, half), BF16),
                jax.ShapeDtypeStruct((10 * CHUNK, half), BF16),
                jax.ShapeDtypeStruct((11 * CHUNK, half), F32),
            ),
            product,
            4 * 10**6,
            grid=(QUARTERS,),
            in_specs=[whole((inner, rows)), half_low, half_left],
            out_specs=tuple(block(n * CHUNK, lambda q: q) for n in (11, 10, 11)),
        )(turned, arrived, arrived)

    first = exchange(outgoing[0], peers)
    turned, expert_rows, first = lax.optimization_barrier((turned, expert_rows, first))
    first, behind = lax.optimization_barrier((first, outgoing[1]))
    second = exchange(behind, peers)
    down_0, up_0, own_0 = partial(first)
    above_0, below_0 = shift(down_0, -1), shift(up_0, 1)
    down_1, up_1, own_1 = partial(second)
    above_1, below_1 = shift(down_1, -1), shift(up_1, 1)
    above_0, below_0, own_1, expert_rows = lax.optimization_barrier((above_0, below_0, own_1, expert_rows))
    returned = exchange(expert_rows, peers)
    hidden_grad = call(
        hidden_grad_kernel,
        jax.ShapeDtypeStruct((rows, inner), BF16),
        2 * product,
        6 * 10**6,
        grid=(QUARTERS,),
        in_specs=[half_low, half_left, block(inner, lambda q: q)]
        + [half_low, half_left, block(inner, lambda q: QUARTERS + q)],
        out_specs=whole((rows, inner)),
        scratch_shapes=[pltpu.VMEM((rows, inner), F32)],
    )(first, first, weight, second, second, weight)

    def combine(returned):
        return call(
            combine_kernel,
            (
                jax.ShapeDtypeStruct((tokens, features), BF16),
                jax.ShapeDtypeStruct((2, tokens), F32),
            ),
            8 * 256 * tokens * features,
            3 * 10**6,
        )(ids, probs, cotangent, returned)

    weight_grad, (layer_out, router_grad) = sum_over_groups(
        ((above_0, below_0, own_0), (above_1, below_1, own_1)), returned, combine
    )
    return (layer_out, router_grad.T, hidden_grad, weight_grad[None])


def solution(mesh):
    in_specs = (
        P(("ep", "dp"), None),
        P(("ep", "dp"), None),
        P(("ep", "dp"), None),
        P(("ep", "dp"), None),
        P("ep", None, None),
    )
    out_specs = (
        P(("ep", "dp"), None),
        P(("ep", "dp"), None),
        P(("ep", "dp"), None),
        P("ep", "dp", None),
    )
    return jax.shard_map(shards, mesh=mesh, in_specs=in_specs, out_specs=out_specs, check_vma=False)
```

```python
import jax
import jax.numpy as jnp
from jax import lax
from jax.experimental import pallas as pl
from jax.experimental.pallas import tpu as pltpu
from jax.sharding import PartitionSpec as P

BF16 = jnp.bfloat16
F32 = jnp.float32
QUARTERS = 4
HALVES = 2
CHUNK = 24
VMEM_BYTES = 20 * 1024 * 1024


def iota(shape, dim):
    return lax.broadcasted_iota(jnp.int32, shape, dim)


def dot(a, b, a_dim=1, b_dim=0):
    return lax.dot_general(a, b, (((a_dim,), (b_dim,)), ((), ())), preferred_element_type=F32)


def onehot(condition):
    return condition.astype(F32).astype(BF16)


def quarter_mask(rows, columns, quarter):
    return (iota((rows, columns), 0) & 3) == quarter


def route_slots(ids):
    tokens = ids.shape[1]
    experts = iota((32, tokens), 0)
    hits = [jnp.where(experts == ids[r : r + 1, :], 1.0, 0.0) for r in range(2)]
    before = onehot(iota((tokens, tokens), 0) < iota((tokens, tokens), 1))
    earlier = dot((hits[0] + hits[1]).astype(BF16), before)
    return [jnp.sum(earlier * hit, axis=0, keepdims=True).astype(jnp.int32) for hit in hits]


def route_masks(ids):
    tokens = ids.shape[1]
    row = iota((256, tokens), 0)
    low, high = [], []
    for r, slot in enumerate(route_slots(ids)):
        expert = ids[r : r + 1, :]
        low.append((row == expert * 8 + slot) & (slot < 8))
        high.append(((row >> 2) == expert * 2 + slot - 8) & (slot >= 8))
    return low, high


def send_kernel(ids_ref, probs_ref, cot_ref, *out_refs):
    low, high = route_masks(ids_ref[...])
    probs = probs_ref[...]

    def weigh(masks):
        weights = [jnp.where(mask, probs[r : r + 1, :], 0.0) for r, mask in enumerate(masks)]
        return jnp.sum(weights[0] + weights[1], axis=1, keepdims=True)

    low_select = onehot(low[0] | low[1])
    high_select = onehot(high[0] | high[1])
    low_weight, high_weight = weigh(low), weigh(high)
    width = cot_ref.shape[1] // (HALVES * QUARTERS)
    for h, out_ref in enumerate(out_refs):
        left = jnp.zeros((256, width), F32)
        for q in range(QUARTERS):
            start = (h * QUARTERS + q) * width
            part = cot_ref[:, start : start + width]
            rows = low_weight * dot(low_select, part)
            out_ref[:, q * width : (q + 1) * width] = rows.astype(BF16)
            left = jnp.where(quarter_mask(256, width, q), dot(high_select, part), left)
        out_ref[:, QUARTERS * width :] = (high_weight * left).astype(BF16)


def expert_kernel(hidden_ref, weight_ref, out_ref, packed_ref, left_ref):
    step = pl.program_id(0)
    rows = hidden_ref.shape[0]
    width = weight_ref.shape[1]

    @pl.when(step == 0)
    def _():
        row, column = iota((256, rows), 0), iota((256, rows), 1)
        peer, place = row >> 3, row & 7
        hidden = hidden_ref[...]
        packed_ref[0:256, :] = dot(onehot(column == peer * 10 + place), hidden).astype(BF16)
        packed_ref[256:512, :] = dot(onehot(column == peer * 10 + 8 + (place >> 2)), hidden).astype(BF16)
        left_ref[...] = jnp.zeros_like(left_ref)

    both = dot(packed_ref[...], weight_ref[...])
    left_ref[...] = jnp.where(quarter_mask(256, width, step), both[256:512, :], left_ref[...])
    out_ref[:, pl.ds(pl.multiple_of(step * width, width), width)] = both[0:256, :].astype(BF16)

    @pl.when(step == QUARTERS - 1)
    def _():
        out_ref[:, QUARTERS * width :] = left_ref[...].astype(BF16)


def natural_rows(low, left, step, rows):
    row, column = iota((rows, 512), 0), iota((rows, 512), 1)
    peer, place = (column & 255) >> 3, column & 7
    in_low = (column < 256) & (row == peer * 10 + place)
    in_left = (column >= 256) & (row == peer * 10 + 8 + (place >> 2)) & ((place & 3) == step)
    return dot(onehot(in_low | in_left), jnp.concatenate([low, left], axis=0)).astype(BF16)


def chunk_order(group, sign, rows):
    block = (rows * 2731) >> 16
    offset = jnp.where(block < 11, 14 - 3 * block, jnp.where(block < 21, 46 - 3 * block, 78 - 3 * block))
    return ((group + sign * offset) & 31) * CHUNK + rows - block * CHUNK


def turn_kernel(place_ref, hidden_ref, turned_ref):
    rows, inner = hidden_ref.shape
    source = chunk_order(place_ref[0], place_ref[1], iota((1, inner), 1))
    select = onehot(iota((inner, inner), 0) == source)
    turned = dot(select, hidden_ref[...], 0, 1).astype(BF16)
    row, column = iota((rows, 256), 0), iota((rows, 256), 1)
    peer, place = column >> 3, column & 7
    turned_ref[:, 0:256] = dot(turned, onehot(row == peer * 10 + place)).astype(BF16)
    left = dot(turned, onehot(row == peer * 10 + 8 + (place >> 2)))
    for q in range(QUARTERS):
        mine = (iota((inner, 256), 1) & 3) == q
        turned_ref[:, (q + 1) * 256 : (q + 2) * 256] = jnp.where(mine, left, 0.0).astype(BF16)


def partial_kernel(scale, turned_ref, turned_left_ref, low_ref, left_ref, down_ref, up_ref, own_ref):
    product = dot(turned_ref[...], low_ref[...]) + dot(turned_left_ref[...], left_ref[...])
    product = product * scale
    down_ref[...] = product[: 11 * CHUNK].astype(BF16)
    up_ref[...] = product[11 * CHUNK : 21 * CHUNK].astype(BF16)
    own_ref[...] = product[21 * CHUNK :]


def shift(block, distance):
    peers, groups = lax.axis_size("ep"), lax.axis_size("dp")
    pairs = [
        (e * groups + i, e * groups + (i + (distance if e % 2 == 0 else -distance)) % groups)
        for e in range(peers)
        for i in range(groups)
    ]
    return lax.ppermute(block, ("ep", "dp"), pairs)


def sum_over_groups(halves, returned, combine):
    def term(k):
        parts = []
        for from_above, from_below, own in halves:
            place = slice(k * CHUNK, (k + 1) * CHUNK)
            total = own[place] + from_above[place].astype(F32)
            if k > 0:
                total += from_below[(k - 1) * CHUNK : k * CHUNK].astype(F32)
            parts.append(total)
        return jnp.concatenate(parts, axis=1)

    rising, falling = term(0), term(10)
    for k in range(1, 5):
        rising, falling = shift(rising.astype(BF16), 3), shift(falling.astype(BF16), -3)
        if k == 4:
            rising, falling, combined = lax.optimization_barrier((rising, falling, combine(returned)))
        rising, falling = rising.astype(F32) + term(k), falling.astype(F32) + term(10 - k)
    rising, falling = shift(rising.astype(BF16), 3), shift(falling.astype(BF16), -3)
    return term(5) + rising.astype(F32) + falling.astype(F32), combined


def hidden_grad_kernel(*refs):
    inputs, (out_ref, total_ref) = refs[:-2], refs[-2:]
    step = pl.program_id(0)
    term = 0.0
    for low_ref, left_ref, weight_ref in zip(inputs[0::3], inputs[1::3], inputs[2::3]):
        rows = natural_rows(low_ref[...], left_ref[...], step, out_ref.shape[0])
        term += dot(rows, weight_ref[...], 1, 1)

    @pl.when(step == 0)
    def _():
        total_ref[...] = term

    @pl.when(step > 0)
    def _():
        total_ref[...] += term

    @pl.when(step == QUARTERS - 1)
    def _():
        out_ref[...] = total_ref[...].astype(BF16)


def combine_kernel(ids_ref, probs_ref, cot_ref, rows_ref, out_ref, grad_ref):
    tokens, features = cot_ref.shape
    width = features // QUARTERS
    low, high = route_masks(ids_ref[...])
    diagonal = iota((tokens, tokens), 0) == iota((tokens, tokens), 1)
    probs = [
        jnp.sum(jnp.where(diagonal, probs_ref[r : r + 1, :], 0.0), axis=1, keepdims=True)
        for r in range(2)
    ]
    left = rows_ref[:, QUARTERS * width :]
    sums = [jnp.zeros((tokens, 1), F32) for _ in range(2)]
    for q in range(QUARTERS):
        part = slice(q * width, (q + 1) * width)
        held = jnp.concatenate([rows_ref[:, part], left], axis=0)
        mine = quarter_mask(256, tokens, q)
        cot = cot_ref[:, part].astype(F32)
        total = jnp.zeros((tokens, width), F32)
        for r in range(2):
            select = jnp.concatenate([onehot(low[r]), onehot(high[r] & mine)], axis=0)
            picked = dot(select, held, 0, 0)
            total += probs[r] * picked
            sums[r] += jnp.sum(cot * picked, axis=1, keepdims=True)
        out_ref[:, part] = total.astype(BF16)
    for r in range(2):
        grad_ref[r : r + 1, :] = (
            jnp.sum(jnp.where(diagonal, sums[r], 0.0), axis=0, keepdims=True) * features ** (-0.5)
        )


def call(kernel, out_shape, flops, bytes_accessed, vmem=VMEM_BYTES, **options):
    return pl.pallas_call(
        kernel,
        out_shape=out_shape,
        compiler_params=pltpu.CompilerParams(vmem_limit_bytes=vmem),
        cost_estimate=pl.CostEstimate(
            flops=flops, bytes_accessed=bytes_accessed, transcendentals=0
        ),
        **options,
    )


def exchange(packed, peers):
    blocks = packed.reshape(peers, packed.shape[0] // peers, packed.shape[1])
    return lax.all_to_all(blocks, "ep", split_axis=0, concat_axis=0, tiled=True).reshape(packed.shape)


def shards(cotangent, route_ids, route_probs, expert_hidden, down_weight):
    peers, groups = lax.axis_size("ep"), lax.axis_size("dp")
    tokens, features = cotangent.shape
    rows, inner = expert_hidden.shape
    weight = down_weight[0]
    ids, probs = route_ids.T, route_probs.T
    width = features // QUARTERS
    packed = jax.ShapeDtypeStruct((256, features + width), BF16)
    product = 2 * rows * inner * features
    whole = lambda shape: pl.BlockSpec(shape, lambda q: (0,) * len(shape))
    column = lambda height: pl.BlockSpec((height, width), lambda q: (0, q))

    half = features // HALVES
    narrow = half // QUARTERS
    half_packed = jax.ShapeDtypeStruct((256, half + narrow), BF16)
    block = lambda height, at: pl.BlockSpec((height, narrow), lambda q: (0, at(q)))
    half_low, half_left = block(256, lambda q: q), block(256, lambda q: QUARTERS)
    outgoing = call(
        send_kernel,
        (half_packed,) * HALVES,
        4 * 256 * tokens * features,
        2 * 10**6,
        60 * 1024 * 1024,
    )(ids, probs, cotangent)
    sign = 1 - 2 * (lax.axis_index("ep") & 1)
    place = jnp.stack([lax.axis_index("dp"), sign]).astype(jnp.int32)
    turned = call(
        turn_kernel,
        jax.ShapeDtypeStruct((inner, 256 * (QUARTERS + 1)), BF16),
        2 * inner * inner * rows,
        10**6,
        in_specs=[pl.BlockSpec(memory_space=pltpu.SMEM), pl.BlockSpec(memory_space=pltpu.VMEM)],
    )(place, expert_hidden)
    expert_rows = call(
        expert_kernel,
        packed,
        2 * product,
        6 * 10**6,
        grid=(QUARTERS,),
        in_specs=[whole((rows, inner)), column(inner)],
        out_specs=whole(packed.shape),
        scratch_shapes=[pltpu.VMEM((512, inner), BF16), pltpu.VMEM((256, width), F32)],
    )(expert_hidden, weight)

    def partial(arrived):
        return call(
            lambda *refs: partial_kernel((groups * rows) ** (-0.5), *refs),
            (
                jax.ShapeDtypeStruct((11 * CHUNK, half), BF16),
                jax.ShapeDtypeStruct((10 * CHUNK, half), BF16),
                jax.ShapeDtypeStruct((11 * CHUNK, half), F32),
            ),
            product,
            4 * 10**6,
            grid=(QUARTERS,),
            in_specs=[
                pl.BlockSpec((inner, 256), lambda q: (0, 0)),
                pl.BlockSpec((inner, 256), lambda q: (0, q + 1)),
                half_low,
                half_left,
            ],
            out_specs=tuple(block(n * CHUNK, lambda q: q) for n in (11, 10, 11)),
        )(turned, turned, arrived, arrived)

    first = exchange(outgoing[0], peers)
    turned, expert_rows, first = lax.optimization_barrier((turned, expert_rows, first))
    first, behind = lax.optimization_barrier((first, outgoing[1]))
    second = exchange(behind, peers)
    down_0, up_0, own_0 = partial(first)
    above_0, below_0 = shift(down_0, -1), shift(up_0, 1)
    down_1, up_1, own_1 = partial(second)
    above_1, below_1 = shift(down_1, -1), shift(up_1, 1)
    above_0, below_0, own_1, expert_rows = lax.optimization_barrier((above_0, below_0, own_1, expert_rows))
    returned = exchange(expert_rows, peers)
    hidden_grad = call(
        hidden_grad_kernel,
        jax.ShapeDtypeStruct((rows, inner), BF16),
        2 * product,
        6 * 10**6,
        grid=(QUARTERS,),
        in_specs=[half_low, half_left, block(inner, lambda q: q)]
        + [half_low, half_left, block(inner, lambda q: QUARTERS + q)],
        out_specs=whole((rows, inner)),
        scratch_shapes=[pltpu.VMEM((rows, inner), F32)],
    )(first, first, weight, second, second, weight)

    def combine(returned):
        return call(
            combine_kernel,
            (
                jax.ShapeDtypeStruct((tokens, features), BF16),
                jax.ShapeDtypeStruct((2, tokens), F32),
            ),
            8 * 256 * tokens * features,
            3 * 10**6,
        )(ids, probs, cotangent, returned)

    weight_grad, (layer_out, router_grad) = sum_over_groups(
        ((above_0, below_0, own_0), (above_1, below_1, own_1)), returned, combine
    )
    return (layer_out, router_grad.T, hidden_grad, weight_grad[None])


def solution(mesh):
    in_specs = (
        P(("ep", "dp"), None),
        P(("ep", "dp"), None),
        P(("ep", "dp"), None),
        P(("ep", "dp"), None),
        P("ep", None, None),
    )
    out_specs = (
        P(("ep", "dp"), None),
        P(("ep", "dp"), None),
        P(("ep", "dp"), None),
        P("ep", "dp", None),
    )
    return jax.shard_map(shards, mesh=mesh, in_specs=in_specs, out_specs=out_specs, check_vma=False)
```

```python
import jax
import jax.numpy as jnp
from jax import lax
from jax.experimental import pallas as pl
from jax.experimental.pallas import tpu as pltpu
from jax.sharding import PartitionSpec as P

BF16 = jnp.bfloat16
F32 = jnp.float32
QUARTERS = 4
HALVES = 2
CHUNK = 24
SENT = 21 * CHUNK
VMEM_BYTES = 20 * 1024 * 1024


def iota(shape, dim):
    return lax.broadcasted_iota(jnp.int32, shape, dim)


def dot(a, b, a_dim=1, b_dim=0):
    return lax.dot_general(a, b, (((a_dim,), (b_dim,)), ((), ())), preferred_element_type=F32)


def onehot(condition):
    return condition.astype(F32).astype(BF16)


def quarter_mask(rows, columns, quarter):
    return (iota((rows, columns), 0) & 3) == quarter


def route_slots(ids):
    tokens = ids.shape[1]
    experts = iota((32, tokens), 0)
    hits = [jnp.where(experts == ids[r : r + 1, :], 1.0, 0.0) for r in range(2)]
    before = onehot(iota((tokens, tokens), 0) < iota((tokens, tokens), 1))
    earlier = dot((hits[0] + hits[1]).astype(BF16), before)
    return [jnp.sum(earlier * hit, axis=0, keepdims=True).astype(jnp.int32) for hit in hits]


def route_masks(ids):
    tokens = ids.shape[1]
    row = iota((256, tokens), 0)
    low, high = [], []
    for r, slot in enumerate(route_slots(ids)):
        expert = ids[r : r + 1, :]
        low.append((row == expert * 8 + slot) & (slot < 8))
        high.append(((row >> 2) == expert * 2 + slot - 8) & (slot >= 8))
    return low, high


def send_kernel(ids_ref, probs_ref, cot_ref, *out_refs):
    low, high = route_masks(ids_ref[...])
    probs = probs_ref[...]

    def weigh(masks):
        weights = [jnp.where(mask, probs[r : r + 1, :], 0.0) for r, mask in enumerate(masks)]
        return jnp.sum(weights[0] + weights[1], axis=1, keepdims=True)

    low_select = onehot(low[0] | low[1])
    high_select = onehot(high[0] | high[1])
    low_weight, high_weight = weigh(low), weigh(high)
    width = cot_ref.shape[1] // (HALVES * QUARTERS)
    for h, out_ref in enumerate(out_refs):
        left = jnp.zeros((256, width), F32)
        for q in range(QUARTERS):
            start = (h * QUARTERS + q) * width
            part = cot_ref[:, start : start + width]
            rows = low_weight * dot(low_select, part)
            out_ref[:, q * width : (q + 1) * width] = rows.astype(BF16)
            left = jnp.where(quarter_mask(256, width, q), dot(high_select, part), left)
        out_ref[:, QUARTERS * width :] = (high_weight * left).astype(BF16)


def expert_kernel(hidden_ref, weight_ref, out_ref, packed_ref, left_ref):
    step = pl.program_id(0)
    rows = hidden_ref.shape[0]
    width = weight_ref.shape[1]

    @pl.when(step == 0)
    def _():
        row, column = iota((256, rows), 0), iota((256, rows), 1)
        peer, place = row >> 3, row & 7
        hidden = hidden_ref[...]
        packed_ref[0:256, :] = dot(onehot(column == peer * 10 + place), hidden).astype(BF16)
        packed_ref[256:512, :] = dot(onehot(column == peer * 10 + 8 + (place >> 2)), hidden).astype(BF16)
        left_ref[...] = jnp.zeros_like(left_ref)

    both = dot(packed_ref[...], weight_ref[...])
    left_ref[...] = jnp.where(quarter_mask(256, width, step), both[256:512, :], left_ref[...])
    out_ref[:, pl.ds(pl.multiple_of(step * width, width), width)] = both[0:256, :].astype(BF16)

    @pl.when(step == QUARTERS - 1)
    def _():
        out_ref[:, QUARTERS * width :] = left_ref[...].astype(BF16)


def natural_rows(low, left, step, rows):
    row, column = iota((rows, 512), 0), iota((rows, 512), 1)
    peer, place = (column & 255) >> 3, column & 7
    in_low = (column < 256) & (row == peer * 10 + place)
    in_left = (column >= 256) & (row == peer * 10 + 8 + (place >> 2)) & ((place & 3) == step)
    return dot(onehot(in_low | in_left), jnp.concatenate([low, left], axis=0)).astype(BF16)


def chunk_order(group, sign, rows):
    block = (rows * 2731) >> 16
    offset = jnp.where(block < 11, 14 - 3 * block, jnp.where(block < 21, 46 - 3 * block, 78 - 3 * block))
    return ((group + sign * offset) & 31) * CHUNK + rows - block * CHUNK


def turn_kernel(place_ref, hidden_ref, sent_ref, own_ref):
    rows, inner = hidden_ref.shape
    source = chunk_order(place_ref[0], place_ref[1], iota((1, inner), 1))
    select = onehot(iota((inner, inner), 0) == source)
    turned = dot(select, hidden_ref[...], 0, 1).astype(BF16)
    row, column = iota((rows, 256), 0), iota((rows, 256), 1)
    peer, place = column >> 3, column & 7
    low = dot(turned, onehot(row == peer * 10 + place))
    left = dot(turned, onehot(row == peer * 10 + 8 + (place >> 2)))
    sent_ref[:, 0:256] = low[:SENT].astype(BF16)
    own_ref[:, 0:256] = low[SENT:].astype(BF16)
    for q in range(QUARTERS):
        mine = jnp.where((iota((inner, 256), 1) & 3) == q, left, 0.0)
        sent_ref[:, (q + 1) * 256 : (q + 2) * 256] = mine[:SENT].astype(BF16)
        own_ref[:, (q + 1) * 256 : (q + 2) * 256] = mine[SENT:].astype(BF16)


def sent_kernel(scale, turned_ref, turned_left_ref, low_ref, left_ref, down_ref, up_ref):
    product = dot(turned_ref[...], low_ref[...]) + dot(turned_left_ref[...], left_ref[...])
    product = product * scale
    down_ref[...] = product[: 11 * CHUNK].astype(BF16)
    up_ref[...] = product[11 * CHUNK :].astype(BF16)


def own_kernel(scale, turned_ref, turned_left_ref, *refs):
    inputs, out_refs = refs[: 2 * HALVES], refs[2 * HALVES :]
    for low_ref, left_ref, out_ref in zip(inputs[0::2], inputs[1::2], out_refs):
        product = dot(turned_ref[...], low_ref[...]) + dot(turned_left_ref[...], left_ref[...])
        out_ref[...] = product * scale


def shift(block, distance):
    peers, groups = lax.axis_size("ep"), lax.axis_size("dp")
    pairs = [
        (e * groups + i, e * groups + (i + (distance if e % 2 == 0 else -distance)) % groups)
        for e in range(peers)
        for i in range(groups)
    ]
    return lax.ppermute(block, ("ep", "dp"), pairs)


def sum_over_groups(halves, returned, combine):
    def term(k):
        parts = []
        for from_above, from_below, own in halves:
            place = slice(k * CHUNK, (k + 1) * CHUNK)
            total = own[place] + from_above[place].astype(F32)
            if k > 0:
                total += from_below[(k - 1) * CHUNK : k * CHUNK].astype(F32)
            parts.append(total)
        return jnp.concatenate(parts, axis=1)

    rising, falling = term(0), term(10)
    for k in range(1, 5):
        rising, falling = shift(rising.astype(BF16), 3), shift(falling.astype(BF16), -3)
        if k == 4:
            rising, falling, combined = lax.optimization_barrier((rising, falling, combine(returned)))
        rising, falling = rising.astype(F32) + term(k), falling.astype(F32) + term(10 - k)
    rising, falling = shift(rising.astype(BF16), 3), shift(falling.astype(BF16), -3)
    return term(5) + rising.astype(F32) + falling.astype(F32), combined


def hidden_grad_kernel(*refs):
    inputs, (out_ref, total_ref) = refs[:-2], refs[-2:]
    step = pl.program_id(0)
    term = 0.0
    for low_ref, left_ref, weight_ref in zip(inputs[0::3], inputs[1::3], inputs[2::3]):
        rows = natural_rows(low_ref[...], left_ref[...], step, out_ref.shape[0])
        term += dot(rows, weight_ref[...], 1, 1)

    @pl.when(step == 0)
    def _():
        total_ref[...] = term

    @pl.when(step > 0)
    def _():
        total_ref[...] += term

    @pl.when(step == QUARTERS - 1)
    def _():
        out_ref[...] = total_ref[...].astype(BF16)


def combine_kernel(ids_ref, probs_ref, cot_ref, rows_ref, out_ref, grad_ref):
    tokens, features = cot_ref.shape
    width = features // QUARTERS
    low, high = route_masks(ids_ref[...])
    diagonal = iota((tokens, tokens), 0) == iota((tokens, tokens), 1)
    probs = [
        jnp.sum(jnp.where(diagonal, probs_ref[r : r + 1, :], 0.0), axis=1, keepdims=True)
        for r in range(2)
    ]
    left = rows_ref[:, QUARTERS * width :]
    sums = [jnp.zeros((tokens, 1), F32) for _ in range(2)]
    for q in range(QUARTERS):
        part = slice(q * width, (q + 1) * width)
        held = jnp.concatenate([rows_ref[:, part], left], axis=0)
        mine = quarter_mask(256, tokens, q)
        cot = cot_ref[:, part].astype(F32)
        total = jnp.zeros((tokens, width), F32)
        for r in range(2):
            select = jnp.concatenate([onehot(low[r]), onehot(high[r] & mine)], axis=0)
            picked = dot(select, held, 0, 0)
            total += probs[r] * picked
            sums[r] += jnp.sum(cot * picked, axis=1, keepdims=True)
        out_ref[:, part] = total.astype(BF16)
    for r in range(2):
        grad_ref[r : r + 1, :] = (
            jnp.sum(jnp.where(diagonal, sums[r], 0.0), axis=0, keepdims=True) * features ** (-0.5)
        )


def call(kernel, out_shape, flops, bytes_accessed, vmem=VMEM_BYTES, **options):
    return pl.pallas_call(
        kernel,
        out_shape=out_shape,
        compiler_params=pltpu.CompilerParams(vmem_limit_bytes=vmem),
        cost_estimate=pl.CostEstimate(
            flops=flops, bytes_accessed=bytes_accessed, transcendentals=0
        ),
        **options,
    )


def exchange(packed, peers):
    blocks = packed.reshape(peers, packed.shape[0] // peers, packed.shape[1])
    return lax.all_to_all(blocks, "ep", split_axis=0, concat_axis=0, tiled=True).reshape(packed.shape)


def shards(cotangent, route_ids, route_probs, expert_hidden, down_weight):
    peers, groups = lax.axis_size("ep"), lax.axis_size("dp")
    tokens, features = cotangent.shape
    rows, inner = expert_hidden.shape
    weight = down_weight[0]
    ids, probs = route_ids.T, route_probs.T
    width = features // QUARTERS
    packed = jax.ShapeDtypeStruct((256, features + width), BF16)
    product = 2 * rows * inner * features
    whole = lambda shape: pl.BlockSpec(shape, lambda q: (0,) * len(shape))
    column = lambda height: pl.BlockSpec((height, width), lambda q: (0, q))

    half = features // HALVES
    narrow = half // QUARTERS
    half_packed = jax.ShapeDtypeStruct((256, half + narrow), BF16)
    block = lambda height, at: pl.BlockSpec((height, narrow), lambda q: (0, at(q)))
    half_low, half_left = block(256, lambda q: q), block(256, lambda q: QUARTERS)
    outgoing = call(
        send_kernel,
        (half_packed,) * HALVES,
        4 * 256 * tokens * features,
        2 * 10**6,
        60 * 1024 * 1024,
    )(ids, probs, cotangent)
    sign = 1 - 2 * (lax.axis_index("ep") & 1)
    place = jnp.stack([lax.axis_index("dp"), sign]).astype(jnp.int32)
    turned_sent, turned_own = call(
        turn_kernel,
        tuple(
            jax.ShapeDtypeStruct((height, 256 * (QUARTERS + 1)), BF16)
            for height in (SENT, inner - SENT)
        ),
        4 * inner * inner * rows,
        2 * 10**6,
        in_specs=[pl.BlockSpec(memory_space=pltpu.SMEM), pl.BlockSpec(memory_space=pltpu.VMEM)],
    )(place, expert_hidden)
    expert_rows = call(
        expert_kernel,
        packed,
        2 * product,
        6 * 10**6,
        grid=(QUARTERS,),
        in_specs=[whole((rows, inner)), column(inner)],
        out_specs=whole(packed.shape),
        scratch_shapes=[pltpu.VMEM((512, inner), BF16), pltpu.VMEM((256, width), F32)],
    )(expert_hidden, weight)

    scale = (groups * rows) ** (-0.5)

    def turned_blocks(height):
        first_columns = pl.BlockSpec((height, 256), lambda q: (0, 0))
        return [first_columns, pl.BlockSpec((height, 256), lambda q: (0, q + 1))]

    def sent(arrived):
        return call(
            lambda *refs: sent_kernel(scale, *refs),
            (
                jax.ShapeDtypeStruct((11 * CHUNK, half), BF16),
                jax.ShapeDtypeStruct((10 * CHUNK, half), BF16),
            ),
            product,
            4 * 10**6,
            grid=(QUARTERS,),
            in_specs=turned_blocks(SENT) + [half_low, half_left],
            out_specs=tuple(block(n * CHUNK, lambda q: q) for n in (11, 10)),
        )(turned_sent, turned_sent, arrived, arrived)

    first = exchange(outgoing[0], peers)
    turned_sent, expert_rows, first = lax.optimization_barrier((turned_sent, expert_rows, first))
    first, behind = lax.optimization_barrier((first, outgoing[1]))
    second = exchange(behind, peers)
    down_0, up_0 = sent(first)
    above_0, below_0 = shift(down_0, -1), shift(up_0, 1)
    down_1, up_1 = sent(second)
    above_1, below_1 = shift(down_1, -1), shift(up_1, 1)
    own_0, own_1 = call(
        lambda *refs: own_kernel(scale, *refs),
        (jax.ShapeDtypeStruct((inner - SENT, half), F32),) * HALVES,
        product,
        4 * 10**6,
        52 * 1024 * 1024,
        grid=(QUARTERS,),
        in_specs=turned_blocks(inner - SENT) + [half_low, half_left] * HALVES,
        out_specs=(block(inner - SENT, lambda q: q),) * HALVES,
    )(turned_own, turned_own, first, first, second, second)
    above_0, below_0, _, expert_rows = lax.optimization_barrier((above_0, below_0, down_1, expert_rows))
    returned = exchange(expert_rows, peers)
    hidden_grad = call(
        hidden_grad_kernel,
        jax.ShapeDtypeStruct((rows, inner), BF16),
        2 * product,
        6 * 10**6,
        grid=(QUARTERS,),
        in_specs=[half_low, half_left, block(inner, lambda q: q)]
        + [half_low, half_left, block(inner, lambda q: QUARTERS + q)],
        out_specs=whole((rows, inner)),
        scratch_shapes=[pltpu.VMEM((rows, inner), F32)],
    )(first, first, weight, second, second, weight)

    def combine(returned):
        return call(
            combine_kernel,
            (
                jax.ShapeDtypeStruct((tokens, features), BF16),
                jax.ShapeDtypeStruct((2, tokens), F32),
            ),
            8 * 256 * tokens * features,
            3 * 10**6,
        )(ids, probs, cotangent, returned)

    weight_grad, (layer_out, router_grad) = sum_over_groups(
        ((above_0, below_0, own_0), (above_1, below_1, own_1)), returned, combine
    )
    return (layer_out, router_grad.T, hidden_grad, weight_grad[None])


def solution(mesh):
    in_specs = (
        P(("ep", "dp"), None),
        P(("ep", "dp"), None),
        P(("ep", "dp"), None),
        P(("ep", "dp"), None),
        P("ep", None, None),
    )
    out_specs = (
        P(("ep", "dp"), None),
        P(("ep", "dp"), None),
        P(("ep", "dp"), None),
        P("ep", "dp", None),
    )
    return jax.shard_map(shards, mesh=mesh, in_specs=in_specs, out_specs=out_specs, check_vma=False)
```

```python
import jax
import jax.numpy as jnp
from jax import lax
from jax.experimental import pallas as pl
from jax.experimental.pallas import tpu as pltpu
from jax.sharding import PartitionSpec as P

BF16 = jnp.bfloat16
F32 = jnp.float32
QUARTERS = 4
HALVES = 2
CHUNK = 24
SENT = 21 * CHUNK
VMEM_BYTES = 20 * 1024 * 1024


def iota(shape, dim):
    return lax.broadcasted_iota(jnp.int32, shape, dim)


def dot(a, b, a_dim=1, b_dim=0):
    return lax.dot_general(a, b, (((a_dim,), (b_dim,)), ((), ())), preferred_element_type=F32)


def onehot(condition):
    return condition.astype(F32).astype(BF16)


def quarter_mask(rows, columns, quarter):
    return (iota((rows, columns), 0) & 3) == quarter


def route_slots(ids):
    tokens = ids.shape[1]
    experts = iota((32, tokens), 0)
    hits = [jnp.where(experts == ids[r : r + 1, :], 1.0, 0.0) for r in range(2)]
    before = onehot(iota((tokens, tokens), 0) < iota((tokens, tokens), 1))
    earlier = dot((hits[0] + hits[1]).astype(BF16), before)
    return [jnp.sum(earlier * hit, axis=0, keepdims=True).astype(jnp.int32) for hit in hits]


def route_masks(ids):
    tokens = ids.shape[1]
    row = iota((256, tokens), 0)
    low, high = [], []
    for r, slot in enumerate(route_slots(ids)):
        expert = ids[r : r + 1, :]
        low.append((row == expert * 8 + slot) & (slot < 8))
        high.append(((row >> 2) == expert * 2 + slot - 8) & (slot >= 8))
    return low, high


def send_kernel(ids_ref, probs_ref, cot_ref, *out_refs):
    low, high = route_masks(ids_ref[...])
    probs = probs_ref[...]

    def weigh(masks):
        weights = [jnp.where(mask, probs[r : r + 1, :], 0.0) for r, mask in enumerate(masks)]
        return jnp.sum(weights[0] + weights[1], axis=1, keepdims=True)

    low_select = onehot(low[0] | low[1])
    high_select = onehot(high[0] | high[1])
    low_weight, high_weight = weigh(low), weigh(high)
    width = cot_ref.shape[1] // (HALVES * QUARTERS)
    for h, out_ref in enumerate(out_refs):
        left = jnp.zeros((256, width), F32)
        for q in range(QUARTERS):
            start = (h * QUARTERS + q) * width
            part = cot_ref[:, start : start + width]
            rows = low_weight * dot(low_select, part)
            out_ref[:, q * width : (q + 1) * width] = rows.astype(BF16)
            left = jnp.where(quarter_mask(256, width, q), dot(high_select, part), left)
        out_ref[:, QUARTERS * width :] = (high_weight * left).astype(BF16)


def expert_kernel(hidden_ref, weight_ref, out_ref, packed_ref, left_ref):
    step = pl.program_id(0)
    rows = hidden_ref.shape[0]
    width = weight_ref.shape[1]

    @pl.when(step == 0)
    def _():
        row, column = iota((256, rows), 0), iota((256, rows), 1)
        peer, place = row >> 3, row & 7
        hidden = hidden_ref[...]
        packed_ref[0:256, :] = dot(onehot(column == peer * 10 + place), hidden).astype(BF16)
        packed_ref[256:512, :] = dot(onehot(column == peer * 10 + 8 + (place >> 2)), hidden).astype(BF16)
        left_ref[...] = jnp.zeros_like(left_ref)

    both = dot(packed_ref[...], weight_ref[...])
    left_ref[...] = jnp.where(quarter_mask(256, width, step), both[256:512, :], left_ref[...])
    out_ref[:, pl.ds(pl.multiple_of(step * width, width), width)] = both[0:256, :].astype(BF16)

    @pl.when(step == QUARTERS - 1)
    def _():
        out_ref[:, QUARTERS * width :] = left_ref[...].astype(BF16)


def natural_rows(low, left, step, rows):
    row, column = iota((rows, 512), 0), iota((rows, 512), 1)
    peer, place = (column & 255) >> 3, column & 7
    in_low = (column < 256) & (row == peer * 10 + place)
    in_left = (column >= 256) & (row == peer * 10 + 8 + (place >> 2)) & ((place & 3) == step)
    return dot(onehot(in_low | in_left), jnp.concatenate([low, left], axis=0)).astype(BF16)


def chunk_order(group, sign, rows):
    block = (rows * 2731) >> 16
    offset = jnp.where(block < 11, 14 - 3 * block, jnp.where(block < 21, 46 - 3 * block, 78 - 3 * block))
    return ((group + sign * offset) & 31) * CHUNK + rows - block * CHUNK


def turn_kernel(place_ref, hidden_ref, sent_ref, own_ref):
    rows, inner = hidden_ref.shape
    source = chunk_order(place_ref[0], place_ref[1], iota((1, inner), 1))
    select = onehot(iota((inner, inner), 0) == source)
    turned = dot(select, hidden_ref[...], 0, 1).astype(BF16)
    row, column = iota((rows, 256), 0), iota((rows, 256), 1)
    peer, place = column >> 3, column & 7
    low = dot(turned, onehot(row == peer * 10 + place))
    left = dot(turned, onehot(row == peer * 10 + 8 + (place >> 2)))
    sent_ref[:, 0:256] = low[:SENT].astype(BF16)
    own_ref[:, 0:256] = low[SENT:].astype(BF16)
    for q in range(QUARTERS):
        mine = jnp.where((iota((inner, 256), 1) & 3) == q, left, 0.0)
        sent_ref[:, (q + 1) * 256 : (q + 2) * 256] = mine[:SENT].astype(BF16)
        own_ref[:, (q + 1) * 256 : (q + 2) * 256] = mine[SENT:].astype(BF16)


def sent_kernel(scale, turned_ref, turned_left_ref, low_ref, left_ref, down_ref, up_ref):
    product = dot(turned_ref[...], low_ref[...]) + dot(turned_left_ref[...], left_ref[...])
    product = product * scale
    down_ref[...] = product[: 11 * CHUNK].astype(BF16)
    up_ref[...] = product[11 * CHUNK :].astype(BF16)


def own_kernel(scale, turned_ref, turned_left_ref, *refs):
    inputs, out_refs = refs[: 2 * HALVES], refs[2 * HALVES :]
    for low_ref, left_ref, out_ref in zip(inputs[0::2], inputs[1::2], out_refs):
        product = dot(turned_ref[...], low_ref[...]) + dot(turned_left_ref[...], left_ref[...])
        out_ref[...] = product * scale


def shift(block, distance):
    peers, groups = lax.axis_size("ep"), lax.axis_size("dp")
    pairs = [
        (e * groups + i, e * groups + (i + (distance if e % 2 == 0 else -distance)) % groups)
        for e in range(peers)
        for i in range(groups)
    ]
    return lax.ppermute(block, ("ep", "dp"), pairs)


def sum_over_groups(halves, returned, combine):
    def term(k):
        parts = []
        for from_above, from_below, own in halves:
            place = slice(k * CHUNK, (k + 1) * CHUNK)
            total = own[place] + from_above[place].astype(F32)
            if k > 0:
                total += from_below[(k - 1) * CHUNK : k * CHUNK].astype(F32)
            parts.append(total)
        return jnp.concatenate(parts, axis=1)

    rising, falling = term(0), term(10)
    for k in range(1, 5):
        rising, falling = shift(rising.astype(BF16), 3), shift(falling.astype(BF16), -3)
        if k == 4:
            falling, combined = lax.optimization_barrier((falling, combine(returned)))
        rising, falling = rising.astype(F32) + term(k), falling.astype(F32) + term(10 - k)
    rising, falling = shift(rising.astype(BF16), 3), shift(falling.astype(BF16), -3)
    return term(5) + rising.astype(F32) + falling.astype(F32), combined


def hidden_grad_kernel(*refs):
    inputs, (out_ref, total_ref) = refs[:-2], refs[-2:]
    step = pl.program_id(0)
    term = 0.0
    for low_ref, left_ref, weight_ref in zip(inputs[0::3], inputs[1::3], inputs[2::3]):
        rows = natural_rows(low_ref[...], left_ref[...], step, out_ref.shape[0])
        term += dot(rows, weight_ref[...], 1, 1)

    @pl.when(step == 0)
    def _():
        total_ref[...] = term

    @pl.when(step > 0)
    def _():
        total_ref[...] += term

    @pl.when(step == QUARTERS - 1)
    def _():
        out_ref[...] = total_ref[...].astype(BF16)


def combine_kernel(ids_ref, probs_ref, cot_ref, rows_ref, out_ref, grad_ref):
    tokens, features = cot_ref.shape
    width = features // QUARTERS
    low, high = route_masks(ids_ref[...])
    diagonal = iota((tokens, tokens), 0) == iota((tokens, tokens), 1)
    probs = [
        jnp.sum(jnp.where(diagonal, probs_ref[r : r + 1, :], 0.0), axis=1, keepdims=True)
        for r in range(2)
    ]
    left = rows_ref[:, QUARTERS * width :]
    sums = [jnp.zeros((tokens, 1), F32) for _ in range(2)]
    for q in range(QUARTERS):
        part = slice(q * width, (q + 1) * width)
        held = jnp.concatenate([rows_ref[:, part], left], axis=0)
        mine = quarter_mask(256, tokens, q)
        cot = cot_ref[:, part].astype(F32)
        total = jnp.zeros((tokens, width), F32)
        for r in range(2):
            select = jnp.concatenate([onehot(low[r]), onehot(high[r] & mine)], axis=0)
            picked = dot(select, held, 0, 0)
            total += probs[r] * picked
            sums[r] += jnp.sum(cot * picked, axis=1, keepdims=True)
        out_ref[:, part] = total.astype(BF16)
    for r in range(2):
        grad_ref[r : r + 1, :] = (
            jnp.sum(jnp.where(diagonal, sums[r], 0.0), axis=0, keepdims=True) * features ** (-0.5)
        )


def call(kernel, out_shape, flops, bytes_accessed, vmem=VMEM_BYTES, **options):
    return pl.pallas_call(
        kernel,
        out_shape=out_shape,
        compiler_params=pltpu.CompilerParams(vmem_limit_bytes=vmem),
        cost_estimate=pl.CostEstimate(
            flops=flops, bytes_accessed=bytes_accessed, transcendentals=0
        ),
        **options,
    )


def exchange(packed, peers):
    blocks = packed.reshape(peers, packed.shape[0] // peers, packed.shape[1])
    return lax.all_to_all(blocks, "ep", split_axis=0, concat_axis=0, tiled=True).reshape(packed.shape)


def shards(cotangent, route_ids, route_probs, expert_hidden, down_weight):
    peers, groups = lax.axis_size("ep"), lax.axis_size("dp")
    tokens, features = cotangent.shape
    rows, inner = expert_hidden.shape
    weight = down_weight[0]
    ids, probs = route_ids.T, route_probs.T
    width = features // QUARTERS
    packed = jax.ShapeDtypeStruct((256, features + width), BF16)
    product = 2 * rows * inner * features
    whole = lambda shape: pl.BlockSpec(shape, lambda q: (0,) * len(shape))
    column = lambda height: pl.BlockSpec((height, width), lambda q: (0, q))

    half = features // HALVES
    narrow = half // QUARTERS
    half_packed = jax.ShapeDtypeStruct((256, half + narrow), BF16)
    block = lambda height, at: pl.BlockSpec((height, narrow), lambda q: (0, at(q)))
    half_low, half_left = block(256, lambda q: q), block(256, lambda q: QUARTERS)
    outgoing = call(
        send_kernel,
        (half_packed,) * HALVES,
        4 * 256 * tokens * features,
        2 * 10**6,
        60 * 1024 * 1024,
    )(ids, probs, cotangent)
    sign = 1 - 2 * (lax.axis_index("ep") & 1)
    place = jnp.stack([lax.axis_index("dp"), sign]).astype(jnp.int32)
    turned_sent, turned_own = call(
        turn_kernel,
        tuple(
            jax.ShapeDtypeStruct((height, 256 * (QUARTERS + 1)), BF16)
            for height in (SENT, inner - SENT)
        ),
        4 * inner * inner * rows,
        2 * 10**6,
        in_specs=[pl.BlockSpec(memory_space=pltpu.SMEM), pl.BlockSpec(memory_space=pltpu.VMEM)],
    )(place, expert_hidden)
    expert_rows = call(
        expert_kernel,
        packed,
        2 * product,
        6 * 10**6,
        grid=(QUARTERS,),
        in_specs=[whole((rows, inner)), column(inner)],
        out_specs=whole(packed.shape),
        scratch_shapes=[pltpu.VMEM((512, inner), BF16), pltpu.VMEM((256, width), F32)],
    )(expert_hidden, weight)

    scale = (groups * rows) ** (-0.5)

    def turned_blocks(height):
        first_columns = pl.BlockSpec((height, 256), lambda q: (0, 0))
        return [first_columns, pl.BlockSpec((height, 256), lambda q: (0, q + 1))]

    def sent(arrived):
        return call(
            lambda *refs: sent_kernel(scale, *refs),
            (
                jax.ShapeDtypeStruct((11 * CHUNK, half), BF16),
                jax.ShapeDtypeStruct((10 * CHUNK, half), BF16),
            ),
            product,
            4 * 10**6,
            grid=(QUARTERS,),
            in_specs=turned_blocks(SENT) + [half_low, half_left],
            out_specs=tuple(block(n * CHUNK, lambda q: q) for n in (11, 10)),
        )(turned_sent, turned_sent, arrived, arrived)

    first = exchange(outgoing[0], peers)
    turned_sent, expert_rows, first = lax.optimization_barrier((turned_sent, expert_rows, first))
    first, behind = lax.optimization_barrier((first, outgoing[1]))
    second = exchange(behind, peers)
    down_0, up_0 = sent(first)
    above_0, below_0 = shift(down_0, -1), shift(up_0, 1)
    down_1, up_1 = sent(second)
    above_1, below_1 = shift(down_1, -1), shift(up_1, 1)
    own_0, own_1 = call(
        lambda *refs: own_kernel(scale, *refs),
        (jax.ShapeDtypeStruct((inner - SENT, half), F32),) * HALVES,
        product,
        4 * 10**6,
        52 * 1024 * 1024,
        grid=(QUARTERS,),
        in_specs=turned_blocks(inner - SENT) + [half_low, half_left] * HALVES,
        out_specs=(block(inner - SENT, lambda q: q),) * HALVES,
    )(turned_own, turned_own, first, first, second, second)
    above_0, below_0, _, expert_rows = lax.optimization_barrier((above_0, below_0, down_1, expert_rows))
    returned = exchange(expert_rows, peers)
    hidden_grad = call(
        hidden_grad_kernel,
        jax.ShapeDtypeStruct((rows, inner), BF16),
        2 * product,
        6 * 10**6,
        grid=(QUARTERS,),
        in_specs=[half_low, half_left, block(inner, lambda q: q)]
        + [half_low, half_left, block(inner, lambda q: QUARTERS + q)],
        out_specs=whole((rows, inner)),
        scratch_shapes=[pltpu.VMEM((rows, inner), F32)],
    )(first, first, weight, second, second, weight)

    def combine(returned):
        return call(
            combine_kernel,
            (
                jax.ShapeDtypeStruct((tokens, features), BF16),
                jax.ShapeDtypeStruct((2, tokens), F32),
            ),
            8 * 256 * tokens * features,
            3 * 10**6,
        )(ids, probs, cotangent, returned)

    weight_grad, (layer_out, router_grad) = sum_over_groups(
        ((above_0, below_0, own_0), (above_1, below_1, own_1)), returned, combine
    )
    return (layer_out, router_grad.T, hidden_grad, weight_grad[None])


def solution(mesh):
    in_specs = (
        P(("ep", "dp"), None),
        P(("ep", "dp"), None),
        P(("ep", "dp"), None),
        P(("ep", "dp"), None),
        P("ep", None, None),
    )
    out_specs = (
        P(("ep", "dp"), None),
        P(("ep", "dp"), None),
        P(("ep", "dp"), None),
        P("ep", "dp", None),
    )
    return jax.shard_map(shards, mesh=mesh, in_specs=in_specs, out_specs=out_specs, check_vma=False)
```

```python
import jax
import jax.numpy as jnp
from jax import lax
from jax.experimental import pallas as pl
from jax.experimental.pallas import tpu as pltpu
from jax.sharding import PartitionSpec as P

BF16 = jnp.bfloat16
F32 = jnp.float32
QUARTERS = 4
HALVES = 2
CHUNK = 24
SENT = 21 * CHUNK
VMEM_BYTES = 20 * 1024 * 1024


def iota(shape, dim):
    return lax.broadcasted_iota(jnp.int32, shape, dim)


def dot(a, b, a_dim=1, b_dim=0):
    return lax.dot_general(a, b, (((a_dim,), (b_dim,)), ((), ())), preferred_element_type=F32)


def onehot(condition):
    return condition.astype(F32).astype(BF16)


def quarter_mask(rows, columns, quarter):
    return (iota((rows, columns), 0) & 3) == quarter


def route_slots(ids):
    tokens = ids.shape[1]
    experts = iota((32, tokens), 0)
    hits = [jnp.where(experts == ids[r : r + 1, :], 1.0, 0.0) for r in range(2)]
    before = onehot(iota((tokens, tokens), 0) < iota((tokens, tokens), 1))
    earlier = dot((hits[0] + hits[1]).astype(BF16), before)
    return [jnp.sum(earlier * hit, axis=0, keepdims=True).astype(jnp.int32) for hit in hits]


def route_masks(ids):
    tokens = ids.shape[1]
    row = iota((256, tokens), 0)
    low, high = [], []
    for r, slot in enumerate(route_slots(ids)):
        expert = ids[r : r + 1, :]
        low.append((row == expert * 8 + slot) & (slot < 8))
        high.append(((row >> 2) == expert * 2 + slot - 8) & (slot >= 8))
    return low, high


def send_kernel(ids_ref, probs_ref, cot_ref, *out_refs):
    low, high = route_masks(ids_ref[...])
    probs = probs_ref[...]

    def weigh(masks):
        weights = [jnp.where(mask, probs[r : r + 1, :], 0.0) for r, mask in enumerate(masks)]
        return jnp.sum(weights[0] + weights[1], axis=1, keepdims=True)

    low_select = onehot(low[0] | low[1])
    high_select = onehot(high[0] | high[1])
    low_weight, high_weight = weigh(low), weigh(high)
    width = cot_ref.shape[1] // (HALVES * QUARTERS)
    for h, out_ref in enumerate(out_refs):
        left = jnp.zeros((256, width), F32)
        for q in range(QUARTERS):
            start = (h * QUARTERS + q) * width
            part = cot_ref[:, start : start + width]
            rows = low_weight * dot(low_select, part)
            out_ref[:, q * width : (q + 1) * width] = rows.astype(BF16)
            left = jnp.where(quarter_mask(256, width, q), dot(high_select, part), left)
        out_ref[:, QUARTERS * width :] = (high_weight * left).astype(BF16)


def expert_kernel(hidden_ref, weight_ref, out_ref, packed_ref, left_ref):
    step = pl.program_id(0)
    rows = hidden_ref.shape[0]
    width = weight_ref.shape[1]

    @pl.when(step == 0)
    def _():
        row, column = iota((256, rows), 0), iota((256, rows), 1)
        peer, place = row >> 3, row & 7
        hidden = hidden_ref[...]
        packed_ref[0:256, :] = dot(onehot(column == peer * 10 + place), hidden).astype(BF16)
        packed_ref[256:512, :] = dot(onehot(column == peer * 10 + 8 + (place >> 2)), hidden).astype(BF16)
        left_ref[...] = jnp.zeros_like(left_ref)

    both = dot(packed_ref[...], weight_ref[...])
    left_ref[...] = jnp.where(quarter_mask(256, width, step), both[256:512, :], left_ref[...])
    out_ref[:, pl.ds(pl.multiple_of(step * width, width), width)] = both[0:256, :].astype(BF16)

    @pl.when(step == QUARTERS - 1)
    def _():
        out_ref[:, QUARTERS * width :] = left_ref[...].astype(BF16)


def natural_rows(low, left, step, rows):
    row, column = iota((rows, 512), 0), iota((rows, 512), 1)
    peer, place = (column & 255) >> 3, column & 7
    in_low = (column < 256) & (row == peer * 10 + place)
    in_left = (column >= 256) & (row == peer * 10 + 8 + (place >> 2)) & ((place & 3) == step)
    return dot(onehot(in_low | in_left), jnp.concatenate([low, left], axis=0)).astype(BF16)


def chunk_order(group, sign, rows):
    block = (rows * 2731) >> 16
    offset = jnp.where(block < 11, 14 - 3 * block, jnp.where(block < 21, 46 - 3 * block, 78 - 3 * block))
    return ((group + sign * offset) & 31) * CHUNK + rows - block * CHUNK


def turn_kernel(place_ref, hidden_ref, sent_ref, own_ref):
    rows, inner = hidden_ref.shape
    source = chunk_order(place_ref[0], place_ref[1], iota((1, inner), 1))
    select = onehot(iota((inner, inner), 0) == source)
    turned = dot(select, hidden_ref[...], 0, 1).astype(BF16)
    row, column = iota((rows, 256), 0), iota((rows, 256), 1)
    peer, place = column >> 3, column & 7
    low = dot(turned, onehot(row == peer * 10 + place))
    left = dot(turned, onehot(row == peer * 10 + 8 + (place >> 2)))
    sent_ref[:, 0:256] = low[:SENT].astype(BF16)
    own_ref[:, 0:256] = low[SENT:].astype(BF16)
    for q in range(QUARTERS):
        mine = jnp.where((iota((inner, 256), 1) & 3) == q, left, 0.0)
        sent_ref[:, (q + 1) * 256 : (q + 2) * 256] = mine[:SENT].astype(BF16)
        own_ref[:, (q + 1) * 256 : (q + 2) * 256] = mine[SENT:].astype(BF16)


def sent_kernel(scale, turned_ref, turned_left_ref, low_ref, left_ref, down_ref, up_ref):
    product = dot(turned_ref[...], low_ref[...]) + dot(turned_left_ref[...], left_ref[...])
    product = product * scale
    down_ref[...] = product[: 11 * CHUNK].astype(BF16)
    up_ref[...] = product[11 * CHUNK :].astype(BF16)


def own_kernel(scale, turned_ref, turned_left_ref, *refs):
    inputs, out_refs = refs[: 2 * HALVES], refs[2 * HALVES :]
    for low_ref, left_ref, out_ref in zip(inputs[0::2], inputs[1::2], out_refs):
        product = dot(turned_ref[...], low_ref[...]) + dot(turned_left_ref[...], left_ref[...])
        out_ref[...] = product * scale


def shift(block, distance):
    peers, groups = lax.axis_size("ep"), lax.axis_size("dp")
    pairs = [
        (e * groups + i, e * groups + (i + (distance if e % 2 == 0 else -distance)) % groups)
        for e in range(peers)
        for i in range(groups)
    ]
    return lax.ppermute(block, ("ep", "dp"), pairs)


def sum_over_groups(halves, returned, combine):
    def term(k):
        parts = []
        for from_above, from_below, own in halves:
            place = slice(k * CHUNK, (k + 1) * CHUNK)
            total = own[place] + from_above[place].astype(F32)
            if k > 0:
                total += from_below[(k - 1) * CHUNK : k * CHUNK].astype(F32)
            parts.append(total)
        return jnp.concatenate(parts, axis=1)

    rising, falling = term(0), term(10)
    for k in range(1, 5):
        rising, falling = shift(rising.astype(BF16), 3), shift(falling.astype(BF16), -3)
        if k == 4:
            falling, combined = lax.optimization_barrier((falling, combine(returned)))
        rising, falling = rising.astype(F32) + term(k), falling.astype(F32) + term(10 - k)
    rising, falling = shift(rising.astype(BF16), 3), shift(falling.astype(BF16), -3)
    return term(5) + rising.astype(F32) + falling.astype(F32), combined


def hidden_grad_kernel(*refs):
    inputs, (out_ref, total_ref) = refs[:-2], refs[-2:]
    step = pl.program_id(0)
    term = 0.0
    for low_ref, left_ref, weight_ref in zip(inputs[0::3], inputs[1::3], inputs[2::3]):
        rows = natural_rows(low_ref[...], left_ref[...], step, out_ref.shape[0])
        term += dot(rows, weight_ref[...], 1, 1)

    @pl.when(step == 0)
    def _():
        total_ref[...] = term

    @pl.when(step > 0)
    def _():
        total_ref[...] += term

    @pl.when(step == QUARTERS - 1)
    def _():
        out_ref[...] = total_ref[...].astype(BF16)


def combine_kernel(ids_ref, probs_ref, cot_ref, rows_ref, out_ref, grad_ref):
    tokens, features = cot_ref.shape
    width = features // QUARTERS
    low, high = route_masks(ids_ref[...])
    diagonal = iota((tokens, tokens), 0) == iota((tokens, tokens), 1)
    probs = [
        jnp.sum(jnp.where(diagonal, probs_ref[r : r + 1, :], 0.0), axis=1, keepdims=True)
        for r in range(2)
    ]
    left = rows_ref[:, QUARTERS * width :]
    sums = [jnp.zeros((tokens, 1), F32) for _ in range(2)]
    for q in range(QUARTERS):
        part = slice(q * width, (q + 1) * width)
        held = jnp.concatenate([rows_ref[:, part], left], axis=0)
        mine = quarter_mask(256, tokens, q)
        cot = cot_ref[:, part].astype(F32)
        total = jnp.zeros((tokens, width), F32)
        for r in range(2):
            select = jnp.concatenate([onehot(low[r]), onehot(high[r] & mine)], axis=0)
            picked = dot(select, held, 0, 0)
            total += probs[r] * picked
            sums[r] += jnp.sum(cot * picked, axis=1, keepdims=True)
        out_ref[:, part] = total.astype(BF16)
    for r in range(2):
        grad_ref[r : r + 1, :] = (
            jnp.sum(jnp.where(diagonal, sums[r], 0.0), axis=0, keepdims=True) * features ** (-0.5)
        )


def call(kernel, out_shape, flops, bytes_accessed, vmem=VMEM_BYTES, **options):
    return pl.pallas_call(
        kernel,
        out_shape=out_shape,
        compiler_params=pltpu.CompilerParams(vmem_limit_bytes=vmem),
        cost_estimate=pl.CostEstimate(
            flops=flops, bytes_accessed=bytes_accessed, transcendentals=0
        ),
        **options,
    )


def exchange(packed, peers):
    blocks = packed.reshape(peers, packed.shape[0] // peers, packed.shape[1])
    return lax.all_to_all(blocks, "ep", split_axis=0, concat_axis=0, tiled=True).reshape(packed.shape)


def shards(cotangent, route_ids, route_probs, expert_hidden, down_weight):
    peers, groups = lax.axis_size("ep"), lax.axis_size("dp")
    tokens, features = cotangent.shape
    rows, inner = expert_hidden.shape
    weight = down_weight[0]
    ids, probs = route_ids.T, route_probs.T
    width = features // QUARTERS
    packed = jax.ShapeDtypeStruct((256, features + width), BF16)
    product = 2 * rows * inner * features
    whole = lambda shape: pl.BlockSpec(shape, lambda q: (0,) * len(shape))
    column = lambda height: pl.BlockSpec((height, width), lambda q: (0, q))

    half = features // HALVES
    narrow = half // QUARTERS
    half_packed = jax.ShapeDtypeStruct((256, half + narrow), BF16)
    block = lambda height, at: pl.BlockSpec((height, narrow), lambda q: (0, at(q)))
    half_low, half_left = block(256, lambda q: q), block(256, lambda q: QUARTERS)
    outgoing = call(
        send_kernel,
        (half_packed,) * HALVES,
        4 * 256 * tokens * features,
        2 * 10**6,
        60 * 1024 * 1024,
    )(ids, probs, cotangent)
    sign = 1 - 2 * (lax.axis_index("ep") & 1)
    place = jnp.stack([lax.axis_index("dp"), sign]).astype(jnp.int32)
    turned_sent, turned_own = call(
        turn_kernel,
        tuple(
            jax.ShapeDtypeStruct((height, 256 * (QUARTERS + 1)), BF16)
            for height in (SENT, inner - SENT)
        ),
        4 * inner * inner * rows,
        2 * 10**6,
        in_specs=[pl.BlockSpec(memory_space=pltpu.SMEM), pl.BlockSpec(memory_space=pltpu.VMEM)],
    )(place, expert_hidden)
    expert_rows = call(
        expert_kernel,
        packed,
        2 * product,
        6 * 10**6,
        grid=(QUARTERS,),
        in_specs=[whole((rows, inner)), column(inner)],
        out_specs=whole(packed.shape),
        scratch_shapes=[pltpu.VMEM((512, inner), BF16), pltpu.VMEM((256, width), F32)],
    )(expert_hidden, weight)

    scale = (groups * rows) ** (-0.5)

    def turned_blocks(height):
        first_columns = pl.BlockSpec((height, 256), lambda q: (0, 0))
        return [first_columns, pl.BlockSpec((height, 256), lambda q: (0, q + 1))]

    def sent(arrived):
        return call(
            lambda *refs: sent_kernel(scale, *refs),
            (
                jax.ShapeDtypeStruct((11 * CHUNK, half), BF16),
                jax.ShapeDtypeStruct((10 * CHUNK, half), BF16),
            ),
            product,
            4 * 10**6,
            grid=(QUARTERS,),
            in_specs=turned_blocks(SENT) + [half_low, half_left],
            out_specs=tuple(block(n * CHUNK, lambda q: q) for n in (11, 10)),
        )(turned_sent, turned_sent, arrived, arrived)

    first = exchange(outgoing[0], peers)
    turned_sent, expert_rows, first = lax.optimization_barrier((turned_sent, expert_rows, first))
    first, behind = lax.optimization_barrier((first, outgoing[1]))
    second = exchange(behind, peers)
    down_0, up_0 = sent(first)
    above_0, below_0 = shift(down_0, -1), shift(up_0, 1)
    down_1, up_1 = sent(second)
    above_1, below_1 = shift(down_1, -1), shift(up_1, 1)
    own_0, own_1 = call(
        lambda *refs: own_kernel(scale, *refs),
        (jax.ShapeDtypeStruct((inner - SENT, half), F32),) * HALVES,
        product,
        4 * 10**6,
        52 * 1024 * 1024,
        grid=(QUARTERS,),
        in_specs=turned_blocks(inner - SENT) + [half_low, half_left] * HALVES,
        out_specs=(block(inner - SENT, lambda q: q),) * HALVES,
    )(turned_own, turned_own, first, first, second, second)
    above_0, below_0, _, expert_rows = lax.optimization_barrier((above_0, below_0, down_1, expert_rows))
    returned = exchange(expert_rows, peers)
    hidden_grad = call(
        hidden_grad_kernel,
        jax.ShapeDtypeStruct((rows, inner), BF16),
        2 * product,
        6 * 10**6,
        56 * 1024 * 1024,
        grid=(QUARTERS,),
        in_specs=[half_low, half_left, block(inner, lambda q: q)]
        + [half_low, half_left, block(inner, lambda q: QUARTERS + q)],
        out_specs=whole((rows, inner)),
        scratch_shapes=[pltpu.VMEM((rows, inner), F32)],
    )(first, first, weight, second, second, weight)

    def combine(returned):
        return call(
            combine_kernel,
            (
                jax.ShapeDtypeStruct((tokens, features), BF16),
                jax.ShapeDtypeStruct((2, tokens), F32),
            ),
            8 * 256 * tokens * features,
            3 * 10**6,
        )(ids, probs, cotangent, returned)

    weight_grad, (layer_out, router_grad) = sum_over_groups(
        ((above_0, below_0, own_0), (above_1, below_1, own_1)), returned, combine
    )
    return (layer_out, router_grad.T, hidden_grad, weight_grad[None])


def solution(mesh):
    in_specs = (
        P(("ep", "dp"), None),
        P(("ep", "dp"), None),
        P(("ep", "dp"), None),
        P(("ep", "dp"), None),
        P("ep", None, None),
    )
    out_specs = (
        P(("ep", "dp"), None),
        P(("ep", "dp"), None),
        P(("ep", "dp"), None),
        P("ep", "dp", None),
    )
    return jax.shard_map(shards, mesh=mesh, in_specs=in_specs, out_specs=out_specs, check_vma=False)
```
